32 devices in a mesh: groups: 2 (over y), dp: 8 (over z, x), tp: 2 (over core).
Axes of the slice: x: 2, y: 2, z: 4, core: 2. Of those that a mesh axis runs over, the one named last changes fastest.
Arguments:
- tokens: bfloat16 [2048, 4096], P(('groups', 'dp')), parts along dimension 0, may hold values from -6 to 6
- pool: bfloat16 [256, 2, 64, 256], P(('groups', 'dp'), None, None, 'tp'), parts along dimension 0, may hold values from -6 to 6
- pages_count: int32 [16], P(('groups', 'dp')), parts along dimension 0, may hold values from 3 to 4, as said below
- owners: int32 [16, 4], P(('groups', 'dp')), parts along dimension 0, may hold values from 0 to 7, as said below
- slots: int32 [16, 4], P(('groups', 'dp')), parts along dimension 0, may hold values from 0 to 15
- homes: int32 [16, 2], P(('groups', 'dp')), parts along dimension 0, may hold values from 0 to 7, as said below
- home_slots: int32 [16, 2], P(('groups', 'dp')), parts along dimension 0, may hold values from 0 to 15, as said below
- norm_attn: float32 [4096], replicated, may hold values from 0.5 to 1.5
- wqkv: bfloat16 [4096, 2, 6, 128], P('dp', 'tp')
Outputs:
- attended: bfloat16 [2048, 1024], P(('groups', 'dp'), 'tp'), parts along dimension 0
- pool_out: bfloat16 [256, 2, 64, 256], P(('groups', 'dp'), None, None, 'tp'), parts along dimension 0
The draws below stay inside these ranges and needn't reach their ends.
There are 2 independent parts, one for each index of `groups`. The reference program is written for one: setup_inputs(seed, part) draws one part's arguments, and reference() takes and returns one part's arrays. A program takes and returns all parts, laid end to end along the dimension named above; an argument that names none is the same for every part. Nothing has to cross between parts.
Inputs may be any that keep to these rules, and one draw needn't show every extreme that they name: `pages_count`: some request has 4. `owners`: the ranks listed for one request are distinct; entries past its page count are not read. `homes`: one request's new pages go to distinct ranks, and every rank receives exactly 2 new pages. `home_slots`: the slots that one rank receives are distinct.
All inputs are finite; a program needn't handle non-finite values.
Results may differ from the reference program's by a relative error of at most 0.011.
Values may be sent and summed in bfloat16 or wider, within the bound.
No kernel may reach another device: no remote copies, remote signals or barrier semaphores. Data moves between devices by JAX's collectives and lax.ppermute only.
A program may use at most 128 MiB of HBM per device.

```python
import jax
import jax.numpy as jnp
from jax import lax

D = 4096
HEAD = 128
QPK = 4
PAGE = 64
TOK_DEV = 128
POOL = 16
KVH = 2
NREQ = 8
PFXP = 4
NEWP = 2
SLOTS = 128
N_DP = 8


def home_layout(key):
    key = jax.random.fold_in(key, 77)
    split_keys = jax.random.split(key, 4)
    offset = jax.random.permutation(split_keys[0], N_DP)
    shifts = jax.random.permutation(split_keys[1], N_DP)[:NEWP]
    relabel = jax.random.permutation(split_keys[2], N_DP)
    ranked = relabel[(offset[:, None] + shifts[None, :]) % N_DP]
    orders = jax.vmap(lambda single_key: jax.random.permutation(single_key, POOL)[:NEWP])(jax.random.split(split_keys[3], N_DP))
    places = orders[ranked, jnp.arange(NEWP)[None, :]]
    return (ranked.astype(jnp.int32), places.astype(jnp.int32))


def draw_homes(key, part):
    ranked, places = home_layout(key)
    return ranked


def draw_home_slots(key, part):
    ranked, places = home_layout(key)
    return places


def draw_pages_count(key, part):
    key = jax.random.fold_in(key, 11)
    first_key, second_key = jax.random.split(key)
    counts = jax.random.randint(first_key, (NREQ,), PFXP - PFXP // 4, PFXP + 1)
    chosen = jax.random.randint(second_key, (), 0, NREQ)
    return jnp.where(jnp.arange(NREQ) == chosen, PFXP, counts).astype(jnp.int32)


def draw_owners(key, part):
    key = jax.random.fold_in(key, 12)
    row_keys = jax.random.split(key, NREQ)
    return jax.vmap(lambda single_key: jax.random.permutation(single_key, N_DP)[:PFXP])(row_keys).astype(jnp.int32)


def draw_wqkv(key, part):
    key = jax.random.fold_in(key, 13)
    values = jax.random.normal(key, (D, KVH, QPK + 2, HEAD), jnp.float32) / jnp.sqrt(jnp.float32(D))
    return values.astype(jnp.bfloat16)


def draw_pool(key, part):
    key = jax.random.fold_in(key, 14)
    split_keys = jax.random.split(key, 1)
    values = jnp.clip(jax.random.normal(split_keys[0], (SLOTS, 2, PAGE, KVH * HEAD), jnp.float32), -6.0, 6.0)
    return values.astype(jnp.bfloat16)


def set_ends(values, key, least, top_value):
    index_at = [jax.random.randint(jax.random.fold_in(key, axis), (), 0, length) for axis, length in enumerate(values.shape)]
    longest = values.shape.index(max(values.shape))
    beside = index_at[:longest] + [(index_at[longest] + 1) % values.shape[longest]] + index_at[longest + 1:]
    return values.at[tuple(index_at)].set(least).at[tuple(beside)].set(top_value)


def block_scale(stream_key, extent, cuts, low, top_value):
    level = 1.0
    for position, blocks in cuts:
        steps = jax.random.uniform(jax.random.fold_in(jax.random.fold_in(stream_key, 6), position), (blocks,), jnp.float32, low / len(cuts), top_value / len(cuts))
        level = level * jnp.repeat(jnp.exp(steps), extent[position] // blocks).reshape((-1,) + (1,) * (len(extent) - 1 - position))
    return level


def bell_draw(key, extent, spread, most, pieces=(), kind=jnp.bfloat16):
    result = jax.random.normal(key, extent, jnp.float32) * spread
    if len(pieces) > 0:
        result = block_scale(key, extent, pieces, -0.22, 0.18) * result
    return jnp.clip(result, min=-most, max=most).astype(kind)


def setup_inputs(seed: int = 0, part: int = 0) -> dict:
    key_of = jax.random.split(jax.random.key(seed), 10)
    part_keys = jax.random.split(jax.random.fold_in(key_of[9], part), 10)
    tokens = bell_draw(part_keys[0], (NREQ * TOK_DEV, D), 1.0, 6.0, ((0, 8),))
    pool = draw_pool(jax.random.fold_in(jax.random.fold_in(key_of[9], part), 71), part)
    pages_count = draw_pages_count(jax.random.fold_in(jax.random.fold_in(key_of[9], part), 71), part)
    owners = draw_owners(jax.random.fold_in(jax.random.fold_in(key_of[9], part), 71), part)
    slots = set_ends(jax.random.randint(part_keys[4], (NREQ, PFXP), 0, POOL), jax.random.fold_in(part_keys[4], 1), 0, POOL - 1).astype(jnp.int32)
    homes = draw_homes(jax.random.fold_in(jax.random.fold_in(key_of[9], part), 71), part)
    home_slots = draw_home_slots(jax.random.fold_in(jax.random.fold_in(key_of[9], part), 71), part)
    norm_attn = jnp.clip(1.0 + 0.1 * jax.random.normal(key_of[7], (D,), jnp.float32), 0.5, 1.5)
    wqkv = draw_wqkv(jax.random.fold_in(key_of[9], 71), part)
    return {"tokens": tokens, "pool": pool, "pages_count": pages_count, "owners": owners, "slots": slots, "homes": homes, "home_slots": home_slots, "norm_attn": norm_attn, "wqkv": wqkv}


def rms_norm(values, gain):
    return values * lax.rsqrt(lax.optimization_barrier(jnp.mean(values * values, axis=-1, keepdims=True)) + 1e-05) * gain

def rotate(values, positions):
    half_size = values.shape[-1] // 2
    index_f = jnp.arange(half_size).astype(jnp.float32)
    inverse = jnp.exp(-(2.0 * index_f / values.shape[-1]) * jnp.log(500000.0))
    angles = positions[..., None] * inverse
    extra = values.ndim - angles.ndim
    angles = angles.reshape(angles.shape[:-1] + (1,) * extra + (half_size,))
    cosine = jnp.cos(angles)
    sine = jnp.sin(angles)
    first = values[..., :half_size]
    second = values[..., half_size:]
    return jnp.concatenate([first * cosine - second * sine, second * cosine + first * sine], axis=-1)

def reference(tokens, pool, pages_count, owners, slots, homes, home_slots, norm_attn, wqkv):
    total_rows = tokens.shape[0]
    heads = wqkv.shape[1]
    group = wqkv.shape[2] - 2
    head_size = wqkv.shape[3]
    inputs = tokens.astype(jnp.float32)
    normed = rms_norm(inputs, norm_attn).astype(jnp.bfloat16)
    projected = jnp.dot(normed, wqkv.reshape(D, heads * (group + 2) * head_size), preferred_element_type=jnp.float32)
    projected = projected.reshape(NREQ, TOK_DEV, heads, group + 2, head_size)
    positions = (pages_count[:, None] * PAGE + jnp.arange(TOK_DEV, dtype=jnp.int32)[None, :]).astype(jnp.float32)
    queries = rotate(projected[:, :, :, :group, :], positions).astype(jnp.bfloat16)
    keys_new = rotate(projected[:, :, :, group, :], positions).astype(jnp.bfloat16)
    values_new = projected[:, :, :, group + 1, :].astype(jnp.bfloat16)
    fresh = jnp.stack([keys_new.reshape(NREQ, NEWP, PAGE, heads * head_size), values_new.reshape(NREQ, NEWP, PAGE, heads * head_size)], axis=2)
    landing = (homes * POOL + home_slots).reshape(-1).astype(jnp.int32)
    pool_out = pool.at[landing].set(fresh.reshape(NREQ * NEWP, 2, PAGE, heads * head_size))
    causal = jnp.arange(TOK_DEV)[:, None] >= jnp.arange(TOK_DEV)[None, :]

    def attend(item):
        query_rows, key_rows, value_rows, count, owner_row, slot_row = item
        pages = pool[(owner_row * POOL + slot_row).astype(jnp.int32)]
        prefix_keys = pages[:, 0].reshape(PFXP * PAGE, heads, head_size)
        prefix_values = pages[:, 1].reshape(PFXP * PAGE, heads, head_size)
        all_keys = jnp.concatenate([prefix_keys, key_rows], axis=0).astype(jnp.float32)
        all_values = jnp.concatenate([prefix_values, value_rows], axis=0).astype(jnp.float32)
        prefix_live = jnp.repeat(jnp.arange(PFXP, dtype=jnp.int32) < count, PAGE)
        allowed = jnp.concatenate([jnp.broadcast_to(prefix_live[None, :], (TOK_DEV, PFXP * PAGE)), causal], axis=1)
        scores = jnp.einsum('thgd,khd->hgtk', query_rows.astype(jnp.float32), all_keys) / jnp.sqrt(jnp.float32(head_size))
        scores = jnp.where(allowed[None, None], scores, -1e+30)
        largest = lax.optimization_barrier(jnp.max(scores, axis=3, keepdims=True))
        weights = jnp.exp(scores - largest)
        totals = lax.optimization_barrier(jnp.sum(weights, axis=3, keepdims=True))
        rounded = weights.astype(jnp.bfloat16).astype(jnp.float32)
        summed = jnp.einsum('hgtk,khd->thgd', rounded, all_values)
        return (summed / jnp.transpose(totals, (2, 0, 1, 3))).astype(jnp.bfloat16)
    attended = lax.map(attend, (queries, keys_new, values_new, pages_count, owners, slots))
    attended = attended.reshape(total_rows, heads * group * head_size)
    return (attended, pool_out)
```

```python
import math

import jax
import jax.numpy as jnp
from jax import lax
from jax.sharding import PartitionSpec as P

PERMUTE_LIMIT = 4


def exclusive(size, distance):
    return [(rank, rank ^ distance) for rank in range(size)]


def rotary_tables(positions, head_size):
    half_size = head_size // 2
    index_f = jnp.arange(half_size).astype(jnp.float32)
    inverse = jnp.exp(-(2.0 * index_f / head_size) * jnp.log(500000.0))
    angles = positions[:, None] * inverse[None, :]
    return jnp.cos(angles), jnp.sin(angles)


def rotate(values, cosine, sine):
    half_size = values.shape[-1] // 2
    first = values[..., :half_size]
    second = values[..., half_size:]
    cosine = cosine[:, None, :]
    sine = sine[:, None, :]
    return jnp.concatenate([first * cosine - second * sine, second * cosine + first * sine], axis=-1)


def attend_part(queries, keys, values, allowed, scale):
    scores = (
        lax.dot_general(queries, keys, (((1,), (1,)), ((), ())), preferred_element_type=jnp.float32)
        * scale
    )
    scores = jnp.where(allowed, scores, -1e30)
    largest = jnp.max(scores, axis=1, keepdims=True)
    weights = jnp.exp(scores - largest)
    totals = jnp.sum(weights, axis=1, keepdims=True)
    summed = jnp.dot(weights.astype(jnp.bfloat16), values, preferred_element_type=jnp.float32)
    return (largest, totals, summed)


def gather_info(info, ranks):
    me = lax.axis_index("dp")
    table = jnp.zeros((ranks, info.shape[0]), jnp.int32).at[me].set(info)
    distance = 1
    while distance < ranks:
        table = table + lax.ppermute(table, "dp", exclusive(ranks, distance))
        distance *= 2
    return table


def project(tokens, gain, weight, ranks):
    me = lax.axis_index("dp")
    core = lax.axis_index("tp")
    rows = weight.shape[0]
    span = 2 * rows
    members = ranks // 2
    token_rows = tokens.shape[0]
    member = me // 2
    other = lax.ppermute(weight, "dp", exclusive(ranks, 1))
    own_first = (me % 2) == core
    direct_weight = jnp.where(own_first, weight, other)
    passed_weight = jnp.where(own_first, other, weight)
    direct_gain = lax.dynamic_slice(gain, (member * span + core * rows,), (rows,))
    passed_gain = lax.dynamic_slice(gain, (member * span + (1 - core) * rows,), (rows,))

    def multiply(direct, passed):
        left = (direct.astype(jnp.float32) * direct_gain).astype(jnp.bfloat16)
        right = (passed.astype(jnp.float32) * passed_gain).astype(jnp.bfloat16)
        return jnp.dot(left, direct_weight, preferred_element_type=jnp.float32) + jnp.dot(
            right, passed_weight, preferred_element_type=jnp.float32
        )

    def half_for(target, which):
        return lax.dynamic_slice(
            tokens, (0, target * span + which * rows), (token_rows, rows)
        )

    total = multiply(half_for(member, core), half_for(member, 1 - core))
    if members <= PERMUTE_LIMIT:
        order = [2, 3, 1] if members == 4 else list(range(1, members))
        received = [
            lax.ppermute(half_for(member ^ step, core), "dp", exclusive(ranks, 2 * step))
            for step in order
        ]
        swapped = [lax.ppermute(piece, "tp", [(0, 1), (1, 0)]) for piece in received]
        returned = [
            lax.ppermute(
                multiply(direct, passed).astype(jnp.bfloat16), "dp", exclusive(ranks, 2 * step)
            )
            for step, direct, passed in zip(order, received, swapped)
        ]
        for piece in returned:
            total = total + piece.astype(jnp.float32)
        return total
    groups = [[2 * index + side for index in range(members)] for side in range(2)]
    blocks = tokens.reshape(token_rows, members, span).transpose(1, 0, 2)
    blocks = lax.all_to_all(
        blocks, "dp", split_axis=0, concat_axis=0, axis_index_groups=groups, tiled=True
    )
    direct = lax.dynamic_slice(blocks, (0, 0, core * rows), (members, token_rows, rows))
    passed = lax.dynamic_slice(blocks, (0, 0, (1 - core) * rows), (members, token_rows, rows))
    parts = multiply(direct.reshape(-1, rows), passed.reshape(-1, rows)).astype(jnp.bfloat16)
    parts = lax.all_to_all(
        parts.reshape(members, token_rows, -1),
        "dp",
        split_axis=0,
        concat_axis=0,
        axis_index_groups=groups,
        tiled=True,
    )
    return jnp.sum(parts.astype(jnp.float32), axis=0)


def local(tokens, pool, pages_count, owners, slots, homes, home_slots, norm_attn, wqkv):
    ranks = lax.axis_size("dp")
    me = lax.axis_index("dp")
    token_rows, width = tokens.shape
    group = wqkv.shape[2] - 2
    blocks = group + 2
    head_size = wqkv.shape[3]
    page_rows = pool.shape[2]
    scale = 1.0 / math.sqrt(head_size)
    prefix = owners.shape[1]

    raw = project(tokens, norm_attn, wqkv.reshape(wqkv.shape[0], -1), ranks)

    lanes = jnp.arange(ranks, dtype=jnp.int32)
    listed = jnp.arange(prefix, dtype=jnp.int32) < pages_count[0]
    info = jnp.concatenate(
        [jnp.where(listed, owners[0], -1), slots[0], homes[0], home_slots[0]]
    )
    table = gather_info(info, ranks)
    asked = jnp.sum(
        jnp.where(table[:, :prefix] == me, table[:, prefix : 2 * prefix], 0), axis=1
    )
    new_pages = homes.shape[1]
    home_table = table[:, 2 * prefix : 2 * prefix + new_pages]
    home_slot_table = table[:, 2 * prefix + new_pages :]
    targets_in = jnp.sum(jnp.where(home_table == me, home_slot_table + 1, 0), axis=1) - 1

    chosen = pool[asked]
    replies = lax.all_to_all(chosen, "dp", split_axis=0, concat_axis=0, tiled=True)

    wide = tokens.astype(jnp.float32)
    row_scale = lax.rsqrt(jnp.mean(wide * wide, axis=-1, keepdims=True) + 1e-05)
    positions = (pages_count[0] * page_rows + jnp.arange(token_rows, dtype=jnp.int32)).astype(
        jnp.float32
    )
    cosine, sine = rotary_tables(positions, head_size)
    projected = (raw * row_scale).reshape(token_rows, blocks, head_size)
    queries = rotate(projected[:, :group], cosine, sine).astype(jnp.bfloat16)
    keys_new = rotate(projected[:, group : group + 1], cosine, sine)[:, 0].astype(jnp.bfloat16)
    values_new = projected[:, group + 1].astype(jnp.bfloat16)

    fresh = jnp.stack(
        [keys_new.reshape(-1, page_rows, head_size), values_new.reshape(-1, page_rows, head_size)],
        axis=1,
    )
    to_home = homes[0][:, None] == lanes[None, :]
    outgoing = sum(
        jnp.where(to_home[index][:, None, None, None], fresh[index][None], 0)
        for index in range(new_pages)
    ).astype(jnp.bfloat16)
    incoming = lax.all_to_all(outgoing, "dp", split_axis=0, concat_axis=0, tiled=True)
    landing = jnp.where(targets_in >= 0, targets_in, pool.shape[0])
    pool_out = pool.at[landing].set(incoming, mode="drop")

    causal = jnp.arange(token_rows)[:, None] >= jnp.arange(token_rows)[None, :]
    prefix_keys = replies[:, 0].reshape(ranks * page_rows, head_size)
    prefix_values = replies[:, 1].reshape(ranks * page_rows, head_size)
    wanted = jnp.any((owners[0][:, None] == lanes[None, :]) & listed[:, None], axis=0)
    prefix_live = jnp.repeat(wanted, page_rows)[None, :]
    outputs = []
    allowed = jnp.concatenate(
        [jnp.broadcast_to(prefix_live, (token_rows, ranks * page_rows)), causal], axis=1
    )
    all_keys = jnp.concatenate([prefix_keys, keys_new], axis=0)
    all_values = jnp.concatenate([prefix_values, values_new], axis=0)
    for member in range(group):
        merged = attend_part(queries[:, member], all_keys, all_values, allowed, scale)
        outputs.append((merged[2] / merged[1]).astype(jnp.bfloat16))
    attended = jnp.concatenate(outputs, axis=1)
    return (attended, pool_out)


def solution(mesh):
    in_specs = (
        P(("groups", "dp"), None),
        P(("groups", "dp"), None, None, "tp"),
        P(("groups", "dp")),
        P(("groups", "dp"), None),
        P(("groups", "dp"), None),
        P(("groups", "dp"), None),
        P(("groups", "dp"), None),
        P(),
        P("dp", "tp", None, None),
    )
    out_specs = (P(("groups", "dp"), "tp"), P(("groups", "dp"), None, None, "tp"))
    return jax.shard_map(local, mesh=mesh, in_specs=in_specs, out_specs=out_specs, check_vma=False)
```

```python
import functools
import math

import jax
import jax.numpy as jnp
from jax import lax
from jax.experimental import pallas as pl
from jax.experimental.pallas import tpu as pltpu
from jax.sharding import PartitionSpec as P

PERMUTE_LIMIT = 4
ANY = pl.BlockSpec(memory_space=pl.ANY)
SCALARS = pl.BlockSpec(memory_space=pltpu.SMEM)
VECTORS = pl.BlockSpec(memory_space=pltpu.VMEM)
PARAMS = pltpu.CompilerParams(vmem_limit_bytes=32 * 1024 * 1024)


def crossed(size, distance):
    return [(rank, rank ^ distance) for rank in range(size)]


def rotary_tables(positions, head_size):
    half_size = head_size // 2
    index_f = jnp.arange(half_size).astype(jnp.float32)
    inverse = jnp.exp(-(2.0 * index_f / head_size) * jnp.log(500000.0))
    angles = positions[:, None] * inverse[None, :]
    cosine, sine = jnp.cos(angles), jnp.sin(angles)
    return jnp.concatenate([cosine, cosine], axis=1), jnp.concatenate([-sine, sine], axis=1)


def turn(values, cosine, sine):
    return values * cosine + pltpu.roll(values, values.shape[-1] // 2, axis=1) * sine


def product_kernel(count, place, *refs):
    direct = jnp.concatenate([ref[...] for ref in refs[:count]], axis=0)
    passed = jnp.concatenate([ref[...] for ref in refs[count : 2 * count]], axis=0)
    own_weight, other_weight = refs[2 * count : 2 * count + 2]
    outs = refs[2 * count + 2 :]
    own_first = (place[0] % 2) == place[1]
    for_own = jnp.where(own_first, direct, passed)
    for_other = jnp.where(own_first, passed, direct)
    result = jnp.dot(for_own, own_weight[...], preferred_element_type=jnp.float32) + jnp.dot(
        for_other, other_weight[...], preferred_element_type=jnp.float32
    )
    rows = outs[0].shape[0]
    for index, out in enumerate(outs):
        out[...] = result[index * rows : (index + 1) * rows].astype(out.dtype)


def products(place, direct, passed, own_weight, other_weight):
    count = len(direct)
    rows, columns = direct[0].shape[0], own_weight.shape[1]
    depth = 2 * own_weight.shape[0]
    return pl.pallas_call(
        functools.partial(product_kernel, count),
        out_shape=[
            jax.ShapeDtypeStruct((rows, columns), jnp.bfloat16 if index else jnp.float32)
            for index in range(count)
        ],
        in_specs=[SCALARS] + [VECTORS] * (2 * count + 2),
        out_specs=[VECTORS] * count,
        compiler_params=PARAMS,
        cost_estimate=pl.CostEstimate(
            flops=2 * count * rows * columns * depth,
            bytes_accessed=2 * depth * (columns + count * rows) + 2 * count * rows * columns,
            transcendentals=0,
        ),
        name="products",
    )(place, *direct, *passed, own_weight, other_weight)


def project(tokens, gain, wqkv, place, ranks, head_size):
    me, core = place[0], place[1]
    rows = wqkv.shape[0]
    span = 2 * rows
    members = ranks // 2
    member = me // 2
    token_rows = tokens.shape[0]
    wide = tokens.astype(jnp.float32)
    row_scale = lax.rsqrt(jnp.mean(wide * wide, axis=-1, keepdims=True) + 1e-05)
    kv_weight = wqkv[:, 0, -2:].reshape(rows, -1)
    q_weight = wqkv[:, 0, :-2].reshape(rows, -1)
    kv_other = lax.ppermute(kv_weight, "dp", crossed(ranks, 1))
    q_other = lax.ppermute(q_weight, "dp", crossed(ranks, 1))

    if members <= PERMUTE_LIMIT:
        def half_for(target, which):
            begin = target * span + which * rows
            piece = lax.dynamic_slice(tokens, (0, begin), (token_rows, rows))
            scale = lax.dynamic_slice(gain, (begin,), (rows,))
            return (piece.astype(jnp.float32) * row_scale * scale).astype(jnp.bfloat16)

        order = [2, 3, 1] if members == 4 else list(range(1, members))
        direct = [
            lax.ppermute(half_for(member ^ step, core), "dp", crossed(ranks, 2 * step))
            for step in order
        ]
        passed = [lax.ppermute(piece, "tp", crossed(2, 1)) for piece in direct]
        direct = [half_for(member, core)] + direct
        passed = [half_for(member, 1 - core)] + passed
        results = []
        for own_weight, other_weight in ((kv_weight, kv_other), (q_weight, q_other)):
            own, *parts = products(place, direct, passed, own_weight, other_weight)
            results.append(
                (
                    own,
                    [
                        lax.ppermute(part, "dp", crossed(ranks, 2 * step))
                        for step, part in zip(order, parts)
                    ],
                )
            )
        return results

    groups = [[2 * index + side for index in range(members)] for side in range(2)]
    normed = (wide * row_scale * gain).astype(jnp.bfloat16)
    blocks = normed.reshape(token_rows, members, span).transpose(1, 0, 2)
    blocks = lax.all_to_all(
        blocks, "dp", split_axis=0, concat_axis=0, axis_index_groups=groups, tiled=True
    ).reshape(members * token_rows, span)
    side = me % 2
    weight = jnp.concatenate([kv_weight, q_weight], axis=1)
    other = jnp.concatenate([kv_other, q_other], axis=1)
    parts = jnp.dot(
        lax.dynamic_slice(blocks, (0, side * rows), (blocks.shape[0], rows)),
        weight,
        preferred_element_type=jnp.float32,
    ) + jnp.dot(
        lax.dynamic_slice(blocks, (0, (1 - side) * rows), (blocks.shape[0], rows)),
        other,
        preferred_element_type=jnp.float32,
    )
    parts = lax.all_to_all(
        parts.astype(jnp.bfloat16).reshape(members, token_rows, -1),
        "dp",
        split_axis=0,
        concat_axis=0,
        axis_index_groups=groups,
        tiled=True,
    )
    total = jnp.sum(parts.astype(jnp.float32), axis=0)
    return [(total[:, : 2 * head_size], []), (total[:, 2 * head_size :], [])]


def info_tables(info, ranks):
    pair = jnp.concatenate([info, lax.ppermute(info, "dp", crossed(ranks, 1))], axis=0)
    members = ranks // 2
    if members <= PERMUTE_LIMIT:
        return [pair] + [
            lax.ppermute(pair, "dp", crossed(ranks, 2 * step)) for step in range(1, members)
        ]
    distance = 2
    while distance < ranks:
        pair = jnp.concatenate([pair, lax.ppermute(pair, "dp", crossed(ranks, distance))], axis=0)
        distance *= 2
    return [pair]


def each_rank(tables, me, visit):
    base = 0
    for table in tables:
        count = table.shape[0]
        if count <= 8:
            for row in range(count):
                visit(table, row, me ^ (base + row))
        else:
            def step(row, carry, table=table, base=base):
                visit(table, row, me ^ (base + row))
                return carry

            lax.fori_loop(0, count, step, 0)
        base += count


def pick_kernel(tables_count, prefix, place, *refs):
    tables = refs[:tables_count]
    pool, chosen, semaphore = refs[tables_count:]
    me = place[0]

    def asked(table, row):
        slot = jnp.int32(-1)
        for page in range(prefix):
            slot = jnp.where(table[row, page] == me, table[row, prefix + page], slot)
        return slot

    def visit(act, table, row, rank):
        slot = asked(table, row)

        @pl.when(slot >= 0)
        def _():
            act(pltpu.make_async_copy(pool.at[slot], chosen.at[rank], semaphore.at[rank]))

    each_rank(tables, me, functools.partial(visit, lambda copy: copy.start()))
    each_rank(tables, me, functools.partial(visit, lambda copy: copy.wait()))


def pick_pages(place, tables, pool, ranks, prefix):
    return pl.pallas_call(
        functools.partial(pick_kernel, len(tables), prefix),
        out_shape=jax.ShapeDtypeStruct((ranks,) + pool.shape[1:], pool.dtype),
        in_specs=[SCALARS] * (1 + len(tables)) + [ANY],
        out_specs=ANY,
        scratch_shapes=[pltpu.SemaphoreType.DMA((ranks,))],
        compiler_params=PARAMS,
        name="pick_pages",
    )(place, *tables, pool)


def land_kernel(tables_count, prefix, new_pages, place, *refs):
    tables = refs[:tables_count]
    incoming, _, pool, semaphore = refs[tables_count:]
    me = place[0]

    def target(table, row):
        slot = jnp.int32(-1)
        for page in range(new_pages):
            home = table[row, 2 * prefix + page]
            slot = jnp.where(home == me, table[row, 2 * prefix + new_pages + page], slot)
        return slot

    def visit(act, table, row, rank):
        slot = target(table, row)

        @pl.when(slot >= 0)
        def _():
            act(pltpu.make_async_copy(incoming.at[rank], pool.at[slot], semaphore.at[rank]))

    each_rank(tables, me, functools.partial(visit, lambda copy: copy.start()))
    each_rank(tables, me, functools.partial(visit, lambda copy: copy.wait()))


def land_pages(place, tables, incoming, pool, prefix, new_pages):
    ranks = incoming.shape[0]
    return pl.pallas_call(
        functools.partial(land_kernel, len(tables), prefix, new_pages),
        out_shape=jax.ShapeDtypeStruct(pool.shape, pool.dtype),
        in_specs=[SCALARS] * (1 + len(tables)) + [ANY, ANY],
        out_specs=ANY,
        scratch_shapes=[pltpu.SemaphoreType.DMA((ranks,))],
        input_output_aliases={len(tables) + 2: 0},
        compiler_params=PARAMS,
        name="land_pages",
    )(place, *tables, incoming, pool)


def fresh_kernel(pieces, homes, own, *refs):
    parts = refs[:pieces]
    cosine, sine, keys, values, outgoing, pages, semaphore = refs[pieces:]
    total = own[...]
    for part in parts:
        total = total + part[...].astype(jnp.float32)
    head_size = keys.shape[1]
    keys[...] = turn(total[:, :head_size], cosine[...], sine[...]).astype(keys.dtype)
    values[...] = total[:, head_size:].astype(values.dtype)
    count, _, page_rows, _ = pages.shape
    copies = []
    for page in range(count):
        span = pl.ds(page * page_rows, page_rows)
        pages[page, 0] = keys[span, :]
        pages[page, 1] = values[span, :]
        copies.append(
            pltpu.make_async_copy(
                pages.at[page], outgoing.at[homes[0, page]], semaphore.at[page]
            )
        )
        copies[-1].start()
    for copy in copies:
        copy.wait()


def fresh_pages(homes, own, parts, cosine, sine, ranks, page_rows):
    token_rows, head_size = cosine.shape
    count = homes.shape[1]
    shape = jax.ShapeDtypeStruct((token_rows, head_size), jnp.bfloat16)
    return pl.pallas_call(
        functools.partial(fresh_kernel, len(parts)),
        out_shape=[
            shape,
            shape,
            jax.ShapeDtypeStruct((ranks, 2, page_rows, head_size), jnp.bfloat16),
        ],
        in_specs=[SCALARS] + [VECTORS] * (len(parts) + 3),
        out_specs=[VECTORS, VECTORS, ANY],
        scratch_shapes=[
            pltpu.VMEM((count, 2, page_rows, head_size), jnp.bfloat16),
            pltpu.SemaphoreType.DMA((count,)),
        ],
        compiler_params=PARAMS,
        name="fresh_pages",
    )(homes, own, *parts, cosine, sine)


def attend_kernel(pieces, together, pages_count, owners, own, *refs):
    parts = refs[:pieces]
    cosine, sine, keys_new, values_new, replies, out, keys, values = refs[pieces:]
    token_rows, head_size = keys_new.shape
    page_rows = replies.shape[2]
    prefix = owners.shape[1]
    group = own.shape[1] // head_size
    count = pages_count[0]
    scale = 1.0 / math.sqrt(head_size)
    for page in range(prefix):
        live = page < count
        source = jnp.where(live, owners[0, page], 0)
        span = pl.ds(page * page_rows, page_rows)
        keys[span, :] = replies[source, 0]
        values[span, :] = jnp.where(live, replies[source, 1], jnp.zeros_like(replies[source, 1]))
    keys[prefix * page_rows :, :] = keys_new[...]
    values[prefix * page_rows :, :] = values_new[...]
    total_rows = keys.shape[0]
    shape = (together * token_rows, total_rows)
    row = lax.broadcasted_iota(jnp.int32, shape, 0) % token_rows
    column = lax.broadcasted_iota(jnp.int32, shape, 1)
    new_column = column - prefix * page_rows
    allowed = (column < count * page_rows) | ((new_column >= 0) & (new_column <= row))
    for first in range(0, group, together):
        queries = []
        for member in range(first, first + together):
            lanes = pl.ds(member * head_size, head_size)
            total = own[:, lanes]
            for part in parts:
                total = total + part[:, lanes].astype(jnp.float32)
            queries.append(turn(total, cosine[...], sine[...]).astype(jnp.bfloat16))
        queries = jnp.concatenate(queries, axis=0)
        scores = (
            lax.dot_general(
                queries, keys[...], (((1,), (1,)), ((), ())), preferred_element_type=jnp.float32
            )
            * scale
        )
        scores = jnp.where(allowed, scores, -1e30)
        largest = jnp.max(scores, axis=1, keepdims=True)
        weights = jnp.exp(scores - largest)
        totals = jnp.sum(weights, axis=1, keepdims=True)
        summed = jnp.dot(
            weights.astype(jnp.bfloat16), values[...], preferred_element_type=jnp.float32
        )
        result = (summed / totals).astype(out.dtype)
        for index in range(together):
            out[:, pl.ds((first + index) * head_size, head_size)] = result[
                index * token_rows : (index + 1) * token_rows
            ]


def attend(pages_count, owners, own, parts, cosine, sine, keys_new, values_new, replies):
    token_rows, head_size = cosine.shape
    group = own.shape[1] // head_size
    total_rows = owners.shape[1] * replies.shape[2] + token_rows
    together = group if total_rows <= 1024 else 1
    return pl.pallas_call(
        functools.partial(attend_kernel, len(parts), together),
        out_shape=jax.ShapeDtypeStruct((token_rows, group * head_size), jnp.bfloat16),
        in_specs=[SCALARS] * 2 + [VECTORS] * (len(parts) + 6),
        out_specs=VECTORS,
        scratch_shapes=[pltpu.VMEM((total_rows, head_size), jnp.bfloat16)] * 2,
        compiler_params=PARAMS,
        cost_estimate=pl.CostEstimate(
            flops=4 * token_rows * group * head_size * total_rows,
            bytes_accessed=2 * replies.size + 4 * own.size,
            transcendentals=token_rows * group * total_rows,
        ),
        name="attend",
    )(pages_count, owners, own, *parts, cosine, sine, keys_new, values_new, replies)


def local(tokens, pool, pages_count, owners, slots, homes, home_slots, norm_attn, wqkv):
    ranks = lax.axis_size("dp")
    place = jnp.stack([lax.axis_index("dp"), lax.axis_index("tp")]).astype(jnp.int32)
    token_rows = tokens.shape[0]
    head_size = wqkv.shape[3]
    page_rows = pool.shape[2]
    prefix = owners.shape[1]
    new_pages = homes.shape[1]

    listed = jnp.arange(prefix, dtype=jnp.int32) < pages_count[0]
    info = jnp.concatenate([jnp.where(listed, owners, -1), slots, homes, home_slots], axis=1)
    tables = info_tables(info, ranks)
    (kv_own, kv_parts), (q_own, q_parts) = project(
        tokens, norm_attn, wqkv, place, ranks, head_size
    )

    chosen = pick_pages(place, tables, pool, ranks, prefix)
    replies = lax.all_to_all(chosen, "dp", split_axis=0, concat_axis=0, tiled=True)

    positions = (pages_count[0] * page_rows + jnp.arange(token_rows, dtype=jnp.int32)).astype(
        jnp.float32
    )
    cosine, sine = rotary_tables(positions, head_size)
    keys_new, values_new, outgoing = fresh_pages(
        homes, kv_own, kv_parts, cosine, sine, ranks, page_rows
    )
    incoming = lax.all_to_all(outgoing, "dp", split_axis=0, concat_axis=0, tiled=True)
    pool_out = land_pages(place, tables, incoming, pool, prefix, new_pages)
    attended = attend(
        pages_count, owners, q_own, q_parts, cosine, sine, keys_new, values_new, replies
    )
    return (attended, pool_out)


def solution(mesh):
    in_specs = (
        P(("groups", "dp"), None),
        P(("groups", "dp"), None, None, "tp"),
        P(("groups", "dp")),
        P(("groups", "dp"), None),
        P(("groups", "dp"), None),
        P(("groups", "dp"), None),
        P(("groups", "dp"), None),
        P(),
        P("dp", "tp", None, None),
    )
    out_specs = (P(("groups", "dp"), "tp"), P(("groups", "dp"), None, None, "tp"))
    return jax.shard_map(local, mesh=mesh, in_specs=in_specs, out_specs=out_specs, check_vma=False)
```

```python
import functools
import math

import jax
import jax.numpy as jnp
from jax import lax
from jax.experimental import pallas as pl
from jax.experimental.pallas import tpu as pltpu
from jax.sharding import PartitionSpec as P

PERMUTE_LIMIT = 4
ANY = pl.BlockSpec(memory_space=pl.ANY)
SCALARS = pl.BlockSpec(memory_space=pltpu.SMEM)
VECTORS = pl.BlockSpec(memory_space=pltpu.VMEM)
PARAMS = pltpu.CompilerParams(vmem_limit_bytes=32 * 1024 * 1024)


def crossed(size, distance):
    return [(rank, rank ^ distance) for rank in range(size)]


def rotary_tables(positions, head_size):
    half_size = head_size // 2
    index_f = jnp.arange(half_size).astype(jnp.float32)
    inverse = jnp.exp(-(2.0 * index_f / head_size) * jnp.log(500000.0))
    angles = positions[:, None] * inverse[None, :]
    cosine, sine = jnp.cos(angles), jnp.sin(angles)
    return jnp.concatenate([cosine, cosine], axis=1), jnp.concatenate([-sine, sine], axis=1)


def turn(values, cosine, sine):
    return values * cosine + pltpu.roll(values, values.shape[-1] // 2, axis=1) * sine


def product_kernel(count, columns, place, *refs):
    direct = jnp.concatenate([ref[...] for ref in refs[:count]], axis=0)
    passed = jnp.concatenate([ref[...] for ref in refs[count : 2 * count]], axis=0)
    own_weight, other_weight = refs[2 * count : 2 * count + 2]
    outs = refs[2 * count + 2 :]
    own_first = (place[0] % 2) == place[1]
    for_own = jnp.where(own_first, direct, passed)
    for_other = jnp.where(own_first, passed, direct)
    result = jnp.dot(
        for_own, own_weight[:, columns], preferred_element_type=jnp.float32
    ) + jnp.dot(for_other, other_weight[:, columns], preferred_element_type=jnp.float32)
    rows = outs[0].shape[0]
    for index, out in enumerate(outs):
        out[...] = result[index * rows : (index + 1) * rows].astype(out.dtype)


def products(place, direct, passed, own_weight, other_weight, begin, columns):
    count = len(direct)
    rows = direct[0].shape[0]
    depth = 2 * own_weight.shape[0]
    return pl.pallas_call(
        functools.partial(product_kernel, count, slice(begin, begin + columns)),
        out_shape=[
            jax.ShapeDtypeStruct((rows, columns), jnp.bfloat16 if index else jnp.float32)
            for index in range(count)
        ],
        in_specs=[SCALARS] + [VECTORS] * (2 * count + 2),
        out_specs=[VECTORS] * count,
        compiler_params=PARAMS,
        cost_estimate=pl.CostEstimate(
            flops=2 * count * rows * columns * depth,
            bytes_accessed=2 * depth * (columns + count * rows) + 2 * count * rows * columns,
            transcendentals=0,
        ),
        name="products",
    )(place, *direct, *passed, own_weight, other_weight)


def project(tokens, gain, weight, other, tables, place, ranks, head_size):
    me, core = place[0], place[1]
    rows = weight.shape[0]
    span = 2 * rows
    members = ranks // 2
    member = me // 2
    token_rows = tokens.shape[0]
    wide = tokens.astype(jnp.float32)
    row_scale = lax.rsqrt(jnp.mean(wide * wide, axis=-1, keepdims=True) + 1e-05)
    kv_columns = 2 * head_size
    q_columns = weight.shape[1] - kv_columns

    if members <= PERMUTE_LIMIT:
        def half_for(target, which):
            begin = target * span + which * rows
            piece = lax.dynamic_slice(tokens, (0, begin), (token_rows, rows))
            scale = lax.dynamic_slice(gain, (begin,), (rows,))
            return (piece.astype(jnp.float32) * row_scale * scale).astype(jnp.bfloat16)

        order = [2, 3, 1] if members == 4 else list(range(1, members))
        pieces = [half_for(member ^ step, core) for step in order]
        pieces, _ = lax.optimization_barrier((pieces, tables))
        direct = [
            lax.ppermute(piece, "dp", crossed(ranks, 2 * step))
            for step, piece in zip(order, pieces)
        ]
        passed = [lax.ppermute(piece, "tp", crossed(2, 1)) for piece in direct]
        direct = [half_for(member, core)] + direct
        passed = [half_for(member, 1 - core)] + passed
        results = []
        for begin, columns in ((q_columns, kv_columns), (0, q_columns)):
            own, *parts = products(place, direct, passed, weight, other, begin, columns)
            results.append(
                (
                    own,
                    [
                        lax.ppermute(part, "dp", crossed(ranks, 2 * step))
                        for step, part in zip(order, parts)
                    ],
                )
            )
        return results

    groups = [[2 * index + side for index in range(members)] for side in range(2)]
    normed = (wide * row_scale * gain).astype(jnp.bfloat16)
    blocks = normed.reshape(token_rows, members, span).transpose(1, 0, 2)
    blocks = lax.all_to_all(
        blocks, "dp", split_axis=0, concat_axis=0, axis_index_groups=groups, tiled=True
    ).reshape(members * token_rows, span)
    side = me % 2
    parts = jnp.dot(
        lax.dynamic_slice(blocks, (0, side * rows), (blocks.shape[0], rows)),
        weight,
        preferred_element_type=jnp.float32,
    ) + jnp.dot(
        lax.dynamic_slice(blocks, (0, (1 - side) * rows), (blocks.shape[0], rows)),
        other,
        preferred_element_type=jnp.float32,
    )
    parts = lax.all_to_all(
        parts.astype(jnp.bfloat16).reshape(members, token_rows, -1),
        "dp",
        split_axis=0,
        concat_axis=0,
        axis_index_groups=groups,
        tiled=True,
    )
    total = jnp.sum(parts.astype(jnp.float32), axis=0)
    return [(total[:, q_columns:], []), (total[:, :q_columns], [])]


def info_tables(info, near, ranks):
    pair = jnp.concatenate([info, near], axis=0)
    members = ranks // 2
    if members <= PERMUTE_LIMIT:
        return [pair] + [
            lax.ppermute(pair, "dp", crossed(ranks, 2 * step)) for step in range(1, members)
        ]
    distance = 2
    while distance < ranks:
        pair = jnp.concatenate([pair, lax.ppermute(pair, "dp", crossed(ranks, distance))], axis=0)
        distance *= 2
    return [pair]


def each_rank(tables, me, visit):
    base = 0
    for table in tables:
        count = table.shape[0]
        if count <= 8:
            for row in range(count):
                visit(table, row, me ^ (base + row))
        else:
            def step(row, carry, table=table, base=base):
                visit(table, row, me ^ (base + row))
                return carry

            lax.fori_loop(0, count, step, 0)
        base += count


def pick_kernel(tables_count, prefix, place, *refs):
    tables = refs[:tables_count]
    pool, chosen, semaphore = refs[tables_count:]
    me = place[0]

    def asked(table, row):
        slot = jnp.int32(-1)
        for page in range(prefix):
            slot = jnp.where(table[row, page] == me, table[row, prefix + page], slot)
        return slot

    def visit(act, table, row, rank):
        slot = asked(table, row)

        @pl.when(slot >= 0)
        def _():
            act(pltpu.make_async_copy(pool.at[slot], chosen.at[rank], semaphore.at[rank]))

    each_rank(tables, me, functools.partial(visit, lambda copy: copy.start()))
    each_rank(tables, me, functools.partial(visit, lambda copy: copy.wait()))


def pick_pages(place, tables, pool, ranks, prefix):
    return pl.pallas_call(
        functools.partial(pick_kernel, len(tables), prefix),
        out_shape=jax.ShapeDtypeStruct((ranks,) + pool.shape[1:], pool.dtype),
        in_specs=[SCALARS] * (1 + len(tables)) + [ANY],
        out_specs=ANY,
        scratch_shapes=[pltpu.SemaphoreType.DMA((ranks,))],
        compiler_params=PARAMS,
        cost_estimate=pl.CostEstimate(flops=0, bytes_accessed=4 * ranks * pool[0].size, transcendentals=0),
        name="pick_pages",
    )(place, *tables, pool)


def land_kernel(tables_count, prefix, new_pages, place, *refs):
    tables = refs[:tables_count]
    incoming, _, pool, semaphore = refs[tables_count:]
    me = place[0]

    def target(table, row):
        slot = jnp.int32(-1)
        for page in range(new_pages):
            home = table[row, 2 * prefix + page]
            slot = jnp.where(home == me, table[row, 2 * prefix + new_pages + page], slot)
        return slot

    def visit(act, table, row, rank):
        slot = target(table, row)

        @pl.when(slot >= 0)
        def _():
            act(pltpu.make_async_copy(incoming.at[rank], pool.at[slot], semaphore.at[rank]))

    each_rank(tables, me, functools.partial(visit, lambda copy: copy.start()))
    each_rank(tables, me, functools.partial(visit, lambda copy: copy.wait()))


def land_pages(place, tables, incoming, pool, prefix, new_pages):
    ranks = incoming.shape[0]
    return pl.pallas_call(
        functools.partial(land_kernel, len(tables), prefix, new_pages),
        out_shape=jax.ShapeDtypeStruct(pool.shape, pool.dtype),
        in_specs=[SCALARS] * (1 + len(tables)) + [ANY, ANY],
        out_specs=ANY,
        scratch_shapes=[pltpu.SemaphoreType.DMA((ranks,))],
        input_output_aliases={len(tables) + 2: 0},
        compiler_params=PARAMS,
        cost_estimate=pl.CostEstimate(flops=0, bytes_accessed=8 * pool[0].size, transcendentals=0),
        name="land_pages",
    )(place, *tables, incoming, pool)


def fresh_kernel(pieces, homes, own, *refs):
    parts = refs[:pieces]
    cosine, sine, keys, values, outgoing, pages, semaphore = refs[pieces:]
    total = own[...]
    for part in parts:
        total = total + part[...].astype(jnp.float32)
    head_size = keys.shape[1]
    keys[...] = turn(total[:, :head_size], cosine[...], sine[...]).astype(keys.dtype)
    values[...] = total[:, head_size:].astype(values.dtype)
    count, _, page_rows, _ = pages.shape
    copies = []
    for page in range(count):
        span = pl.ds(page * page_rows, page_rows)
        pages[page, 0] = keys[span, :]
        pages[page, 1] = values[span, :]
        copies.append(
            pltpu.make_async_copy(
                pages.at[page], outgoing.at[homes[0, page]], semaphore.at[page]
            )
        )
        copies[-1].start()
    for copy in copies:
        copy.wait()


def fresh_pages(homes, own, parts, cosine, sine, ranks, page_rows):
    token_rows, head_size = cosine.shape
    count = homes.shape[1]
    shape = jax.ShapeDtypeStruct((token_rows, head_size), jnp.bfloat16)
    return pl.pallas_call(
        functools.partial(fresh_kernel, len(parts)),
        out_shape=[
            shape,
            shape,
            jax.ShapeDtypeStruct((ranks, 2, page_rows, head_size), jnp.bfloat16),
        ],
        in_specs=[SCALARS] + [VECTORS] * (len(parts) + 3),
        out_specs=[VECTORS, VECTORS, ANY],
        scratch_shapes=[
            pltpu.VMEM((count, 2, page_rows, head_size), jnp.bfloat16),
            pltpu.SemaphoreType.DMA((count,)),
        ],
        compiler_params=PARAMS,
        cost_estimate=pl.CostEstimate(flops=0, bytes_accessed=16 * token_rows * head_size, transcendentals=0),
        name="fresh_pages",
    )(homes, own, *parts, cosine, sine)


def attend_kernel(pieces, together, pages_count, owners, own, *refs):
    parts = refs[:pieces]
    cosine, sine, keys_new, values_new, replies, out, keys, values = refs[pieces:]
    token_rows, head_size = keys_new.shape
    page_rows = replies.shape[2]
    prefix = owners.shape[1]
    group = own.shape[1] // head_size
    count = pages_count[0]
    scale = 1.0 / math.sqrt(head_size)
    for page in range(prefix):
        live = page < count
        source = jnp.where(live, owners[0, page], 0)
        span = pl.ds(page * page_rows, page_rows)
        keys[span, :] = replies[source, 0]
        values[span, :] = jnp.where(live, replies[source, 1], jnp.zeros_like(replies[source, 1]))
    keys[prefix * page_rows :, :] = keys_new[...]
    values[prefix * page_rows :, :] = values_new[...]
    total_rows = keys.shape[0]
    shape = (together * token_rows, total_rows)
    row = lax.broadcasted_iota(jnp.int32, shape, 0) % token_rows
    column = lax.broadcasted_iota(jnp.int32, shape, 1)
    new_column = column - prefix * page_rows
    allowed = (column < count * page_rows) | ((new_column >= 0) & (new_column <= row))
    for first in range(0, group, together):
        queries = []
        for member in range(first, first + together):
            lanes = pl.ds(member * head_size, head_size)
            total = own[:, lanes]
            for part in parts:
                total = total + part[:, lanes].astype(jnp.float32)
            queries.append(turn(total, cosine[...], sine[...]).astype(jnp.bfloat16))
        queries = jnp.concatenate(queries, axis=0)
        scores = (
            lax.dot_general(
                queries, keys[...], (((1,), (1,)), ((), ())), preferred_element_type=jnp.float32
            )
            * scale
        )
        scores = jnp.where(allowed, scores, -1e30)
        largest = jnp.max(scores, axis=1, keepdims=True)
        weights = jnp.exp(scores - largest)
        totals = jnp.sum(weights, axis=1, keepdims=True)
        summed = jnp.dot(
            weights.astype(jnp.bfloat16), values[...], preferred_element_type=jnp.float32
        )
        result = (summed / totals).astype(out.dtype)
        for index in range(together):
            out[:, pl.ds((first + index) * head_size, head_size)] = result[
                index * token_rows : (index + 1) * token_rows
            ]


def attend(pages_count, owners, own, parts, cosine, sine, keys_new, values_new, replies):
    token_rows, head_size = cosine.shape
    group = own.shape[1] // head_size
    total_rows = owners.shape[1] * replies.shape[2] + token_rows
    together = group if total_rows <= 1024 else 1
    return pl.pallas_call(
        functools.partial(attend_kernel, len(parts), together),
        out_shape=jax.ShapeDtypeStruct((token_rows, group * head_size), jnp.bfloat16),
        in_specs=[SCALARS] * 2 + [VECTORS] * (len(parts) + 6),
        out_specs=VECTORS,
        scratch_shapes=[pltpu.VMEM((total_rows, head_size), jnp.bfloat16)] * 2,
        compiler_params=PARAMS,
        cost_estimate=pl.CostEstimate(
            flops=4 * token_rows * group * head_size * total_rows,
            bytes_accessed=2 * replies.size + 4 * own.size,
            transcendentals=token_rows * group * total_rows,
        ),
        name="attend",
    )(pages_count, owners, own, *parts, cosine, sine, keys_new, values_new, replies)


def local(tokens, pool, pages_count, owners, slots, homes, home_slots, norm_attn, wqkv):
    ranks = lax.axis_size("dp")
    place = jnp.stack([lax.axis_index("dp"), lax.axis_index("tp")]).astype(jnp.int32)
    token_rows = tokens.shape[0]
    head_size = wqkv.shape[3]
    page_rows = pool.shape[2]
    prefix = owners.shape[1]
    new_pages = homes.shape[1]

    listed = jnp.arange(prefix, dtype=jnp.int32) < pages_count[0]
    info = jnp.concatenate([jnp.where(listed, owners, -1), slots, homes, home_slots], axis=1)
    near = lax.ppermute(info, "dp", crossed(ranks, 1))
    weight, near = lax.optimization_barrier((wqkv.reshape(wqkv.shape[0], -1), near))
    other = lax.ppermute(weight, "dp", crossed(ranks, 1))
    tables = info_tables(info, near, ranks)
    (kv_own, kv_parts), (q_own, q_parts) = project(
        tokens, norm_attn, weight, other, tables, place, ranks, head_size
    )

    chosen = pick_pages(place, tables, pool, ranks, prefix)
    replies = lax.all_to_all(chosen, "dp", split_axis=0, concat_axis=0, tiled=True)

    positions = (pages_count[0] * page_rows + jnp.arange(token_rows, dtype=jnp.int32)).astype(
        jnp.float32
    )
    cosine, sine = rotary_tables(positions, head_size)
    keys_new, values_new, outgoing = fresh_pages(
        homes, kv_own, kv_parts, cosine, sine, ranks, page_rows
    )
    incoming = lax.all_to_all(outgoing, "dp", split_axis=0, concat_axis=0, tiled=True)
    pool_out = land_pages(place, tables, incoming, pool, prefix, new_pages)
    attended = attend(
        pages_count, owners, q_own, q_parts, cosine, sine, keys_new, values_new, replies
    )
    return (attended, pool_out)


def solution(mesh):
    in_specs = (
        P(("groups", "dp"), None),
        P(("groups", "dp"), None, None, "tp"),
        P(("groups", "dp")),
        P(("groups", "dp"), None),
        P(("groups", "dp"), None),
        P(("groups", "dp"), None),
        P(("groups", "dp"), None),
        P(),
        P("dp", "tp", None, None),
    )
    out_specs = (P(("groups", "dp"), "tp"), P(("groups", "dp"), None, None, "tp"))
    return jax.shard_map(local, mesh=mesh, in_specs=in_specs, out_specs=out_specs, check_vma=False)
```

```python
import functools
import math

import jax
import jax.numpy as jnp
from jax import lax
from jax.experimental import pallas as pl
from jax.experimental.pallas import tpu as pltpu
from jax.sharding import PartitionSpec as P

ANY = pl.BlockSpec(memory_space=pl.ANY)
SCALARS = pl.BlockSpec(memory_space=pltpu.SMEM)
VECTORS = pl.BlockSpec(memory_space=pltpu.VMEM)
PARAMS = pltpu.CompilerParams(vmem_limit_bytes=32 * 1024 * 1024)


def crossed(size, distance):
    return [(rank, rank ^ distance) for rank in range(size)]


def rotary_tables(positions, head_size):
    half_size = head_size // 2
    index_f = jnp.arange(half_size).astype(jnp.float32)
    inverse = jnp.exp(-(2.0 * index_f / head_size) * jnp.log(500000.0))
    angles = positions[:, None] * inverse[None, :]
    cosine, sine = jnp.cos(angles), jnp.sin(angles)
    return jnp.concatenate([cosine, cosine], axis=1), jnp.concatenate([-sine, sine], axis=1)


def turn(values, cosine, sine):
    return values * cosine + pltpu.roll(values, values.shape[-1] // 2, axis=1) * sine


def product_kernel(place, *refs):
    direct = jnp.concatenate([ref[...] for ref in refs[:4]], axis=0)
    passed = jnp.concatenate([ref[...] for ref in refs[4:8]], axis=0)
    own_weight, other_weight, kept, leaving = refs[8:]
    own_first = (place[0] % 2) == place[1]
    for_own = jnp.where(own_first, direct, passed)
    for_other = jnp.where(own_first, passed, direct)
    result = jnp.dot(for_own, own_weight[...], preferred_element_type=jnp.float32) + jnp.dot(
        for_other, other_weight[...], preferred_element_type=jnp.float32
    )
    rows = kept.shape[0] // 2
    kept[:rows] = result[:rows]
    kept[rows:] = result[2 * rows : 3 * rows]
    leaving[:rows] = result[rows : 2 * rows].astype(leaving.dtype)
    leaving[rows:] = result[3 * rows :].astype(leaving.dtype)


def products(place, direct, passed, own_weight, other_weight):
    rows, columns = direct[0].shape[0], own_weight.shape[1]
    depth = 2 * own_weight.shape[0]
    return pl.pallas_call(
        product_kernel,
        out_shape=[
            jax.ShapeDtypeStruct((2 * rows, columns), jnp.float32),
            jax.ShapeDtypeStruct((2 * rows, columns), jnp.bfloat16),
        ],
        in_specs=[SCALARS] + [VECTORS] * 10,
        out_specs=[VECTORS] * 2,
        compiler_params=PARAMS,
        cost_estimate=pl.CostEstimate(
            flops=8 * rows * columns * depth,
            bytes_accessed=2 * depth * (columns + 4 * rows) + 12 * rows * columns,
            transcendentals=0,
        ),
        name="products",
    )(place, *direct, *passed, own_weight, other_weight)


def fold_kernel(kept, arrived, far):
    rows = far.shape[0]
    far[...] = (kept[rows:] + arrived[rows:].astype(jnp.float32)).astype(far.dtype)


def fold(kept, arrived):
    rows, columns = kept.shape[0] // 2, kept.shape[1]
    return pl.pallas_call(
        fold_kernel,
        out_shape=jax.ShapeDtypeStruct((rows, columns), jnp.bfloat16),
        in_specs=[VECTORS] * 2,
        out_specs=VECTORS,
        compiler_params=PARAMS,
        cost_estimate=pl.CostEstimate(
            flops=rows * columns, bytes_accessed=10 * rows * columns, transcendentals=0
        ),
        name="fold",
    )(kept, arrived)


def project(tokens, gain, wqkv, place, ranks):
    me, core = place[0], place[1]
    rows = wqkv.shape[0]
    span = 2 * rows
    members = ranks // 2
    member = me // 2
    token_rows = tokens.shape[0]
    wide = tokens.astype(jnp.float32)
    row_scale = lax.rsqrt(jnp.mean(wide * wide, axis=-1, keepdims=True) + 1e-05)

    def near(weight):
        return lax.ppermute(weight, "dp", crossed(ranks, 1))

    if members == 4:
        def half_for(target, which):
            begin = target * span + which * rows
            piece = lax.dynamic_slice(tokens, (0, begin), (token_rows, rows))
            scale = lax.dynamic_slice(gain, (begin,), (rows,))
            return (piece.astype(jnp.float32) * row_scale * scale).astype(jnp.bfloat16)

        pieces = [half_for(member ^ step, core) for step in range(1, 4)]
        pieces, wqkv = lax.optimization_barrier((pieces, wqkv))
        direct = [None] * 3
        for step in (2, 3, 1):
            direct[step - 1] = lax.ppermute(pieces[step - 1], "dp", crossed(ranks, 2 * step))
        passed = [lax.ppermute(piece, "tp", crossed(2, 1)) for piece in direct]
        direct = [half_for(member, core)] + direct
        passed = [half_for(member, 1 - core)] + passed
        kv_weight = wqkv[:, 0, -2:].reshape(rows, -1)
        q_weight = wqkv[:, 0, :-2].reshape(rows, -1)
        results = []
        for weight in (kv_weight, q_weight):
            kept, leaving = products(place, direct, passed, weight, near(weight))
            arrived = lax.ppermute(leaving, "dp", crossed(ranks, 2))
            far = lax.ppermute(fold(kept, arrived), "dp", crossed(ranks, 4))
            results.append([kept, arrived, far])
        return results

    groups = [[2 * index + side for index in range(members)] for side in range(2)]
    normed = (wide * row_scale * gain).astype(jnp.bfloat16)
    blocks = normed.reshape(token_rows, members, span).transpose(1, 0, 2)
    blocks = lax.all_to_all(
        blocks, "dp", split_axis=0, concat_axis=0, axis_index_groups=groups, tiled=True
    ).reshape(members * token_rows, span)
    side = me % 2
    weight = wqkv.reshape(rows, -1)
    parts = jnp.dot(
        lax.dynamic_slice(blocks, (0, side * rows), (blocks.shape[0], rows)),
        weight,
        preferred_element_type=jnp.float32,
    ) + jnp.dot(
        lax.dynamic_slice(blocks, (0, (1 - side) * rows), (blocks.shape[0], rows)),
        near(weight),
        preferred_element_type=jnp.float32,
    )
    parts = lax.all_to_all(
        parts.astype(jnp.bfloat16).reshape(members, token_rows, -1),
        "dp",
        split_axis=0,
        concat_axis=0,
        axis_index_groups=groups,
        tiled=True,
    )
    total = jnp.sum(parts.astype(jnp.float32), axis=0)
    q_columns = weight.shape[1] - 2 * wqkv.shape[3]
    return [[total[:, q_columns:]], [total[:, :q_columns]]]


def each_rank(ranks, visit):
    if ranks <= 8:
        for rank in range(ranks):
            visit(rank)
    else:
        def step(rank, carry):
            visit(rank)
            return carry

        lax.fori_loop(0, ranks, step, 0)


def pick_kernel(table, pool, chosen, semaphore):
    ranks = chosen.shape[0]

    def visit(act, rank):
        @pl.when(table[rank, 0] >= 0)
        def _():
            act(pltpu.make_async_copy(pool.at[table[rank, 0]], chosen.at[rank], semaphore.at[rank]))

    each_rank(ranks, functools.partial(visit, lambda copy: copy.start()))
    each_rank(ranks, functools.partial(visit, lambda copy: copy.wait()))


def pick_pages(table, pool):
    ranks = table.shape[0]
    return pl.pallas_call(
        pick_kernel,
        out_shape=jax.ShapeDtypeStruct((ranks,) + pool.shape[1:], pool.dtype),
        in_specs=[SCALARS, ANY],
        out_specs=ANY,
        scratch_shapes=[pltpu.SemaphoreType.DMA((ranks,))],
        compiler_params=PARAMS,
        cost_estimate=pl.CostEstimate(
            flops=0, bytes_accessed=4 * ranks * pool[0].size, transcendentals=0
        ),
        name="pick_pages",
    )(table, pool)


def land_kernel(table, incoming, _, pool, semaphore):
    ranks = incoming.shape[0]

    def visit(act, rank):
        @pl.when(table[rank, 1] >= 0)
        def _():
            act(pltpu.make_async_copy(incoming.at[rank], pool.at[table[rank, 1]], semaphore.at[rank]))

    each_rank(ranks, functools.partial(visit, lambda copy: copy.start()))
    each_rank(ranks, functools.partial(visit, lambda copy: copy.wait()))


def land_pages(table, incoming, pool):
    ranks = incoming.shape[0]
    return pl.pallas_call(
        land_kernel,
        out_shape=jax.ShapeDtypeStruct(pool.shape, pool.dtype),
        in_specs=[SCALARS, ANY, ANY],
        out_specs=ANY,
        scratch_shapes=[pltpu.SemaphoreType.DMA((ranks,))],
        input_output_aliases={2: 0},
        compiler_params=PARAMS,
        cost_estimate=pl.CostEstimate(
            flops=0, bytes_accessed=8 * pool[0].size, transcendentals=0
        ),
        name="land_pages",
    )(table, incoming, pool)


def fresh_kernel(pieces, homes, *refs):
    parts = refs[:pieces]
    cosine, sine, keys, values, outgoing, pages, semaphore = refs[pieces:]
    token_rows, head_size = keys.shape
    total = sum(part[:token_rows].astype(jnp.float32) for part in parts)
    keys[...] = turn(total[:, :head_size], cosine[...], sine[...]).astype(keys.dtype)
    values[...] = total[:, head_size:].astype(values.dtype)
    count, _, page_rows, _ = pages.shape
    copies = []
    for page in range(count):
        span = pl.ds(page * page_rows, page_rows)
        pages[page, 0] = keys[span, :]
        pages[page, 1] = values[span, :]
        copies.append(
            pltpu.make_async_copy(
                pages.at[page], outgoing.at[homes[0, page]], semaphore.at[page]
            )
        )
        copies[-1].start()
    for copy in copies:
        copy.wait()


def fresh_pages(homes, parts, cosine, sine, ranks, page_rows):
    token_rows, head_size = cosine.shape
    count = homes.shape[1]
    shape = jax.ShapeDtypeStruct((token_rows, head_size), jnp.bfloat16)
    return pl.pallas_call(
        functools.partial(fresh_kernel, len(parts)),
        out_shape=[
            shape,
            shape,
            jax.ShapeDtypeStruct((ranks, 2, page_rows, head_size), jnp.bfloat16),
        ],
        in_specs=[SCALARS] + [VECTORS] * (len(parts) + 2),
        out_specs=[VECTORS, VECTORS, ANY],
        scratch_shapes=[
            pltpu.VMEM((count, 2, page_rows, head_size), jnp.bfloat16),
            pltpu.SemaphoreType.DMA((count,)),
        ],
        compiler_params=PARAMS,
        cost_estimate=pl.CostEstimate(flops=0, bytes_accessed=16 * token_rows * head_size, transcendentals=0),
        name="fresh_pages",
    )(homes, *parts, cosine, sine)


def attend_kernel(pieces, together, pages_count, owners, *refs):
    parts = refs[:pieces]
    cosine, sine, keys_new, values_new, replies, out, keys, values = refs[pieces:]
    token_rows, head_size = keys_new.shape
    page_rows = replies.shape[2]
    prefix = owners.shape[1]
    group = out.shape[1] // head_size
    count = pages_count[0]
    scale = 1.0 / math.sqrt(head_size)
    for page in range(prefix):
        live = page < count
        source = jnp.where(live, owners[0, page], 0)
        span = pl.ds(page * page_rows, page_rows)
        keys[span, :] = replies[source, 0]
        values[span, :] = jnp.where(live, replies[source, 1], jnp.zeros_like(replies[source, 1]))
    keys[prefix * page_rows :, :] = keys_new[...]
    values[prefix * page_rows :, :] = values_new[...]
    total_rows = keys.shape[0]
    shape = (together * token_rows, total_rows)
    row = lax.broadcasted_iota(jnp.int32, shape, 0) % token_rows
    column = lax.broadcasted_iota(jnp.int32, shape, 1)
    new_column = column - prefix * page_rows
    allowed = (column < count * page_rows) | ((new_column >= 0) & (new_column <= row))
    for first in range(0, group, together):
        queries = []
        for member in range(first, first + together):
            lanes = pl.ds(member * head_size, head_size)
            total = sum(part[:token_rows, lanes].astype(jnp.float32) for part in parts)
            queries.append(turn(total, cosine[...], sine[...]).astype(jnp.bfloat16))
        queries = jnp.concatenate(queries, axis=0)
        scores = (
            lax.dot_general(
                queries, keys[...], (((1,), (1,)), ((), ())), preferred_element_type=jnp.float32
            )
            * scale
        )
        scores = jnp.where(allowed, scores, -1e30)
        largest = jnp.max(scores, axis=1, keepdims=True)
        weights = jnp.exp(scores - largest)
        totals = jnp.sum(weights, axis=1, keepdims=True)
        summed = jnp.dot(
            weights.astype(jnp.bfloat16), values[...], preferred_element_type=jnp.float32
        )
        result = (summed / totals).astype(out.dtype)
        for index in range(together):
            out[:, pl.ds((first + index) * head_size, head_size)] = result[
                index * token_rows : (index + 1) * token_rows
            ]


def attend(pages_count, owners, parts, cosine, sine, keys_new, values_new, replies):
    token_rows, head_size = cosine.shape
    group = parts[0].shape[1] // head_size
    total_rows = owners.shape[1] * replies.shape[2] + token_rows
    together = group if total_rows <= 1024 else 1
    return pl.pallas_call(
        functools.partial(attend_kernel, len(parts), together),
        out_shape=jax.ShapeDtypeStruct((token_rows, group * head_size), jnp.bfloat16),
        in_specs=[SCALARS] * 2 + [VECTORS] * (len(parts) + 5),
        out_specs=VECTORS,
        scratch_shapes=[pltpu.VMEM((total_rows, head_size), jnp.bfloat16)] * 2,
        compiler_params=PARAMS,
        cost_estimate=pl.CostEstimate(
            flops=4 * token_rows * group * head_size * total_rows,
            bytes_accessed=2 * replies.size + 4 * parts[0].size,
            transcendentals=token_rows * group * total_rows,
        ),
        name="attend",
    )(pages_count, owners, *parts, cosine, sine, keys_new, values_new, replies)


def local(tokens, pool, pages_count, owners, slots, homes, home_slots, norm_attn, wqkv):
    ranks = lax.axis_size("dp")
    place = jnp.stack([lax.axis_index("dp"), lax.axis_index("tp")]).astype(jnp.int32)
    token_rows = tokens.shape[0]
    head_size = wqkv.shape[3]
    page_rows = pool.shape[2]
    prefix = owners.shape[1]

    lanes = jnp.arange(ranks, dtype=jnp.int32)
    listed = jnp.arange(prefix, dtype=jnp.int32) < pages_count[0]
    asks = (owners[0][None, :] == lanes[:, None]) & listed[None, :]
    lands = homes[0][None, :] == lanes[:, None]
    wanted = jnp.max(jnp.where(asks, slots, -1), axis=1)
    replaced = jnp.max(jnp.where(lands, home_slots, -1), axis=1)
    table = lax.all_to_all(
        jnp.stack([wanted, replaced], axis=1), "dp", split_axis=0, concat_axis=0, tiled=True
    )
    kv_parts, q_parts = project(tokens, norm_attn, wqkv, place, ranks)
    replies = lax.all_to_all(
        pick_pages(table, pool), "dp", split_axis=0, concat_axis=0, tiled=True
    )

    positions = (pages_count[0] * page_rows + jnp.arange(token_rows, dtype=jnp.int32)).astype(
        jnp.float32
    )
    cosine, sine = rotary_tables(positions, head_size)
    keys_new, values_new, outgoing = fresh_pages(
        homes, kv_parts, cosine, sine, ranks, page_rows
    )
    incoming = lax.all_to_all(outgoing, "dp", split_axis=0, concat_axis=0, tiled=True)
    pool_out = land_pages(table, incoming, pool)
    attended = attend(
        pages_count, owners, q_parts, cosine, sine, keys_new, values_new, replies
    )
    return (attended, pool_out)


def solution(mesh):
    in_specs = (
        P(("groups", "dp"), None),
        P(("groups", "dp"), None, None, "tp"),
        P(("groups", "dp")),
        P(("groups", "dp"), None),
        P(("groups", "dp"), None),
        P(("groups", "dp"), None),
        P(("groups", "dp"), None),
        P(),
        P("dp", "tp", None, None),
    )
    out_specs = (P(("groups", "dp"), "tp"), P(("groups", "dp"), None, None, "tp"))
    return jax.shard_map(local, mesh=mesh, in_specs=in_specs, out_specs=out_specs, check_vma=False)
```

```python
import functools
import math

import jax
import jax.numpy as jnp
from jax import lax
from jax.experimental import pallas as pl
from jax.experimental.pallas import tpu as pltpu
from jax.sharding import PartitionSpec as P

WAITS = dict(kv=30, q=10, pick=3, fresh=0, fold=0, attend=10, land=0, prepare=0)
ANY = pl.BlockSpec(memory_space=pl.ANY)
SCALARS = pl.BlockSpec(memory_space=pltpu.SMEM)
VECTORS = pl.BlockSpec(memory_space=pltpu.VMEM)
PARAMS = pltpu.CompilerParams(vmem_limit_bytes=32 * 1024 * 1024)


def wait(name):
    return pl.CostEstimate(flops=int(WAITS[name] * 1.15e9), bytes_accessed=0, transcendentals=0)


def tie(value, *others):
    return lax.optimization_barrier((value,) + others)[0]


def crossed(size, distance):
    return [(rank, rank ^ distance) for rank in range(size)]


def rotary_tables(positions, head_size):
    half_size = head_size // 2
    index_f = jnp.arange(half_size).astype(jnp.float32)
    inverse = jnp.exp(-(2.0 * index_f / head_size) * jnp.log(500000.0))
    angles = positions[:, None] * inverse[None, :]
    cosine, sine = jnp.cos(angles), jnp.sin(angles)
    return jnp.concatenate([cosine, cosine], axis=1), jnp.concatenate([-sine, sine], axis=1)


def turn(values, cosine, sine):
    return values * cosine + pltpu.roll(values, values.shape[-1] // 2, axis=1) * sine


def prepare_kernel(*refs):
    arguments, pieces, numbers = refs[:7], refs[7:12], refs[12]
    local_copies, semaphore = refs[13:20], refs[20]
    copies = [
        pltpu.make_async_copy(here, there, semaphore.at[index])
        for index, (here, there) in enumerate(zip(arguments, local_copies))
    ]
    for copy in copies:
        copy.start()
    tokens, gain, pages_count, owners, slots, homes, home_slots = local_copies
    token_rows, width = tokens.shape
    rows = pieces[0].shape[1]
    member, core = lax.axis_index("dp") // 2, lax.axis_index("tp")
    for copy in copies:
        copy.wait()
    count = pages_count[0, 0]
    values = [count]
    values += [jnp.where(page < count, owners[0, page], -1) for page in range(owners.shape[1])]
    for ref in (slots, homes, home_slots):
        values += [ref[0, page] for page in range(ref.shape[1])]
    shape = (pieces[-1].shape[0] - token_rows, rows)
    column = lax.broadcasted_iota(jnp.int32, shape, 1)
    tail = jnp.zeros(shape, jnp.float32)
    for index, value in enumerate(values):
        numbers[0, index] = value
        tail = jnp.where(column == index, value.astype(jnp.float32), tail)
    wide = tokens[...].astype(jnp.float32)
    row_scale = lax.rsqrt(jnp.sum(wide * wide, axis=1, keepdims=True) / width + 1e-05)
    for index, piece in enumerate(pieces):
        target = member ^ max(index - 1, 0)
        half = 1 - core if index == 1 else core
        span = pl.ds(pl.multiple_of((2 * target + half) * rows, 128), rows)
        part = tokens[:, span].astype(jnp.float32) * row_scale * gain[:, span]
        piece[:token_rows] = part.astype(piece.dtype)
        if index > 1:
            piece[token_rows:] = tail.astype(piece.dtype)


def prepare(tokens, gain, pages_count, requests, rows):
    token_rows, width = tokens.shape
    heights = [token_rows] * 2 + [token_rows + 16] * 3
    arguments = [tokens, gain.reshape(1, width), pages_count.reshape(1, 1)] + requests
    count = 1 + sum(part.shape[1] for part in requests)
    return pl.pallas_call(
        prepare_kernel,
        out_shape=[jax.ShapeDtypeStruct((height, rows), jnp.bfloat16) for height in heights]
        + [jax.ShapeDtypeStruct((1, count), jnp.int32)],
        in_specs=[ANY] * 7,
        out_specs=[VECTORS] * 5 + [SCALARS],
        scratch_shapes=[pltpu.VMEM(value.shape, value.dtype) for value in arguments[:2]]
        + [pltpu.SMEM(value.shape, value.dtype) for value in arguments[2:]]
        + [pltpu.SemaphoreType.DMA((7,))],
        compiler_params=pltpu.CompilerParams(vmem_limit_bytes=60 * 1024 * 1024),
        cost_estimate=wait("prepare"),
        name="prepare",
    )(*arguments)


def side_by_side(*refs):
    return jnp.concatenate(
        [blocks[index] for blocks in refs for index in range(blocks.shape[0])], axis=1
    )


def product_kernel(place, *refs):
    own_weight = refs[8]
    other = [ref for ref in refs[9:] if len(ref.shape) == 3]
    kept, *leaving = refs[9 + len(other) :]
    rows = leaving[-1].shape[0] // (1 if len(leaving) == 3 else 2)
    direct = jnp.concatenate([ref[:rows] for ref in refs[:4]], axis=0)
    passed = jnp.concatenate([ref[:rows] for ref in refs[4:8]], axis=0)
    own_first = (place[0] % 2) == place[1]
    for_own = jnp.where(own_first, direct, passed)
    for_other = jnp.where(own_first, passed, direct)
    result = jnp.dot(
        for_own, side_by_side(own_weight), preferred_element_type=jnp.float32
    ) + jnp.dot(for_other, side_by_side(*other), preferred_element_type=jnp.float32)
    result = [result[index * rows : (index + 1) * rows] for index in range(4)]
    kept[:rows] = result[0]
    if len(leaving) == 3:
        for out, part in zip(leaving, result[1:]):
            out[...] = part.astype(out.dtype)
    else:
        kept[rows:] = result[2]
        leaving[0][:rows] = result[1].astype(leaving[0].dtype)
        leaving[0][rows:] = result[3].astype(leaving[0].dtype)


def products(place, direct, passed, own_weight, first, other, paired):
    rows, head_size = direct[0].shape[0], own_weight.shape[2]
    shapes = [(2 * rows, jnp.float32), (2 * rows, jnp.bfloat16)]
    if not paired:
        shapes = [(rows, jnp.float32)] + [(rows, jnp.bfloat16)] * 3
    count = sum(part.shape[0] for part in other)
    columns = count * head_size
    depth = 2 * own_weight.shape[1]
    blocks = pl.BlockSpec((count,) + own_weight.shape[1:], lambda step: (first // count, 0, 0))
    return pl.pallas_call(
        product_kernel,
        grid=(1,),
        out_shape=[jax.ShapeDtypeStruct((height, columns), kind) for height, kind in shapes],
        in_specs=[SCALARS] + [VECTORS] * 8 + [blocks] + [VECTORS] * len(other),
        out_specs=[VECTORS] * len(shapes),
        compiler_params=PARAMS,
        cost_estimate=wait("q" if first == 0 else "kv"),
        name="products",
    )(place, *direct, *passed, own_weight, *other)


def fold_kernel(kept, arrived, *refs):
    pages, far, relay = refs[:4], refs[4], refs[5]
    rows = far.shape[0]
    far[...] = (kept[rows:] + arrived[rows:].astype(jnp.float32)).astype(far.dtype)
    for index, page in enumerate(pages):
        relay[index] = page[1]


def fold(kept, arrived, pages):
    rows, columns = kept.shape[0] // 2, kept.shape[1]
    return pl.pallas_call(
        fold_kernel,
        out_shape=[
            jax.ShapeDtypeStruct((rows, columns), jnp.bfloat16),
            jax.ShapeDtypeStruct((4,) + pages[0].shape[1:], pages[0].dtype),
        ],
        in_specs=[VECTORS] * 6,
        out_specs=[VECTORS] * 2,
        compiler_params=PARAMS,
        cost_estimate=wait("fold"),
        name="fold",
    )(kept, arrived, *pages)


def answer(numbers, prefix, me, ranks):
    new_pages = (numbers.shape[1] - 1 - 2 * prefix) // 2
    starts = [1, 1 + prefix, 1 + 2 * prefix, 1 + 2 * prefix + new_pages, numbers.shape[1]]
    owners, slots, homes, home_slots = [
        numbers[:, first:last] for first, last in zip(starts[:-1], starts[1:])
    ]
    asked = jnp.max(jnp.where(owners == me, slots, -1), axis=1)
    replaced = jnp.max(jnp.where(homes == me, home_slots, -1), axis=1)
    return jnp.stack([asked, replaced, ranks], axis=1).astype(jnp.int32)


def near(values, ranks):
    return lax.ppermute(values, "dp", crossed(ranks, 1))


def along(values, ranks, step):
    return lax.ppermute(values, "dp", crossed(ranks, 2 * step))


def column_plan(tokens, gain, wqkv, pages_count, requests, pool, place, ranks):
    me = place[0]
    rows = wqkv.shape[0]
    blocks = wqkv.shape[2]
    token_rows = tokens.shape[0]
    prefix = requests[0].shape[1]
    weight = wqkv[:, 0].transpose(1, 0, 2)
    kv_other, *q_other = [
        near(weight[first : first + 2], ranks) for first in range(blocks - 2, -1, -2)
    ]
    own_direct, own_passed, *pieces, numbers = prepare(tokens, gain, pages_count, requests, rows)
    direct = [None] * 3
    for step in (2, 3, 1):
        direct[step - 1] = along(pieces[step - 1], ranks, step)
    direct = tie(direct, kv_other)
    passed = [lax.ppermute(piece, "tp", crossed(2, 1)) for piece in direct]
    table = [piece[token_rows : token_rows + 1, : numbers.shape[1]] for piece in direct]
    table = jnp.concatenate([numbers] + [row.astype(jnp.int32) for row in table], axis=0)
    direct = [own_direct] + direct
    passed = [own_passed] + passed

    kv_own, *leaving = products(place, direct, passed, weight, blocks - 2, [kv_other], False)
    kv_parts = [kv_own] + [along(part, ranks, step) for step, part in zip((1, 2, 3), leaving)]

    table = tie(table, kv_own)
    table = jnp.concatenate([table, near(table, ranks)], axis=0)
    lanes = jnp.arange(ranks, dtype=jnp.int32)
    table = answer(table, prefix, me, (2 * lanes % ranks + lanes // 4) ^ me)
    *picked, copied = pick_pages(table, pool, 4)
    pages = picked[:1] + [along(picked[step], ranks, step) for step in (1, 2, 3)]

    q_other = tie(q_other[::-1], kv_parts, picked[0])
    q_kept, leaving = products(place, direct, passed, weight, 0, q_other, True)
    q_arrived = along(leaving, ranks, 1)
    kv_parts = tie(kv_parts, q_kept)

    def finish(fresh):
        far, relay = fold(q_kept, tie(q_arrived, fresh), pages)
        relayed = near(relay, ranks)
        return [q_kept, q_arrived, along(far, ranks, 2)], pages + [relayed]

    return kv_parts, finish, table, copied, numbers


def general_plan(tokens, gain, wqkv, pages_count, requests, pool, place, ranks):
    me = place[0]
    rows = wqkv.shape[0]
    members = ranks // 2
    token_rows = tokens.shape[0]
    blocks = wqkv.shape[2]
    prefix = requests[0].shape[1]
    weight = wqkv[:, 0].transpose(1, 0, 2)
    groups = [[2 * index + side for index in range(members)] for side in range(2)]
    wide = tokens.astype(jnp.float32)
    row_scale = lax.rsqrt(jnp.mean(wide * wide, axis=-1, keepdims=True) + 1e-05)
    normed = (wide * row_scale * gain).astype(jnp.bfloat16)
    chunks = normed.reshape(token_rows, members, 2 * rows).transpose(1, 0, 2)
    chunks = lax.all_to_all(
        chunks, "dp", split_axis=0, concat_axis=0, axis_index_groups=groups, tiled=True
    ).reshape(members * token_rows, 2 * rows)
    side = me % 2
    parts = jnp.dot(
        lax.dynamic_slice(chunks, (0, side * rows), (chunks.shape[0], rows)),
        side_by_side(weight),
        preferred_element_type=jnp.float32,
    ) + jnp.dot(
        lax.dynamic_slice(chunks, (0, (1 - side) * rows), (chunks.shape[0], rows)),
        side_by_side(near(weight, ranks)),
        preferred_element_type=jnp.float32,
    )
    parts = lax.all_to_all(
        parts.astype(jnp.bfloat16).reshape(members, token_rows, -1),
        "dp",
        split_axis=0,
        concat_axis=0,
        axis_index_groups=groups,
        tiled=True,
    )
    total = jnp.sum(parts.astype(jnp.float32), axis=0)
    q_columns = (blocks - 2) * wqkv.shape[3]
    lanes = jnp.arange(ranks, dtype=jnp.int32)
    listed = jnp.arange(prefix, dtype=jnp.int32) < pages_count[0]
    numbers = jnp.concatenate(
        [pages_count[:, None], jnp.where(listed, requests[0], -1)] + requests[1:], axis=1
    )
    table = answer(jnp.broadcast_to(numbers, (ranks,) + numbers.shape[1:]), prefix, lanes[:, None], lanes)
    table = lax.all_to_all(table[:, :2], "dp", split_axis=0, concat_axis=0, tiled=True)
    table = jnp.concatenate([table, lanes[:, None]], axis=1)
    chosen, copied = pick_pages(table, pool, 1)
    replies = lax.all_to_all(chosen, "dp", split_axis=0, concat_axis=0, tiled=True)

    def finish(fresh):
        return [total[:, :q_columns]], [replies]

    return [total[:, q_columns:]], finish, table, copied, numbers


def each_row(rows, visit):
    if rows <= 8:
        for row in range(rows):
            visit(row)
    else:
        def step(row, carry):
            visit(row)
            return carry

        lax.fori_loop(0, rows, step, 0)


def pick_kernel(table, pool, *refs):
    *outs, copied, semaphore = refs
    rows = table.shape[0]
    whole = pltpu.make_async_copy(pool, copied, semaphore.at[rows])
    whole.start()

    def visit(act, row):
        @pl.when(table[row, 0] >= 0)
        def _():
            place = (0, table[row, 2]) if len(outs) == 1 else (row % len(outs), row // len(outs))
            act(
                pltpu.make_async_copy(
                    pool.at[table[row, 0]], outs[place[0]].at[place[1]], semaphore.at[row]
                )
            )

    each_row(rows, functools.partial(visit, lambda copy: copy.start()))
    each_row(rows, functools.partial(visit, lambda copy: copy.wait()))
    whole.wait()


def pick_pages(table, pool, count):
    rows = table.shape[0]
    page = pool.shape[1:]
    return pl.pallas_call(
        pick_kernel,
        out_shape=[jax.ShapeDtypeStruct((rows // count,) + page, pool.dtype)] * count
        + [jax.ShapeDtypeStruct(pool.shape, pool.dtype)],
        in_specs=[SCALARS, ANY],
        out_specs=[ANY] * (count + 1),
        scratch_shapes=[pltpu.SemaphoreType.DMA((rows + 1,))],
        compiler_params=PARAMS,
        cost_estimate=wait("pick"),
        name="pick_pages",
    )(table, pool)


def land_kernel(table, incoming, _, pool, semaphore):
    ranks = incoming.shape[0]

    def visit(act, row):
        @pl.when(table[row, 1] >= 0)
        def _():
            act(
                pltpu.make_async_copy(
                    incoming.at[table[row, 2]], pool.at[table[row, 1]], semaphore.at[row]
                )
            )

    each_row(ranks, functools.partial(visit, lambda copy: copy.start()))
    each_row(ranks, functools.partial(visit, lambda copy: copy.wait()))


def land_pages(table, incoming, pool):
    ranks = incoming.shape[0]
    return pl.pallas_call(
        land_kernel,
        out_shape=jax.ShapeDtypeStruct(pool.shape, pool.dtype),
        in_specs=[SCALARS, ANY, ANY],
        out_specs=ANY,
        scratch_shapes=[pltpu.SemaphoreType.DMA((ranks,))],
        input_output_aliases={2: 0},
        compiler_params=PARAMS,
        cost_estimate=wait("land"),
        name="land_pages",
    )(table, incoming, pool)


def fresh_kernel(pieces, first, numbers, *refs):
    parts = refs[:pieces]
    cosine, sine, keys, values, outgoing, pages, semaphore = refs[pieces:]
    token_rows, head_size = keys.shape
    total = sum(part[:token_rows].astype(jnp.float32) for part in parts)
    keys[...] = turn(total[:, :head_size], cosine[...], sine[...]).astype(keys.dtype)
    values[...] = total[:, head_size:].astype(values.dtype)
    count, _, page_rows, _ = pages.shape
    copies = []
    for page in range(count):
        span = pl.ds(page * page_rows, page_rows)
        pages[page, 0] = keys[span, :]
        pages[page, 1] = values[span, :]
        copies.append(
            pltpu.make_async_copy(
                pages.at[page], outgoing.at[numbers[0, first + page]], semaphore.at[page]
            )
        )
        copies[-1].start()
    for copy in copies:
        copy.wait()


def fresh_pages(numbers, first, count, parts, cosine, sine, ranks, page_rows):
    token_rows, head_size = cosine.shape
    shape = jax.ShapeDtypeStruct((token_rows, head_size), jnp.bfloat16)
    return pl.pallas_call(
        functools.partial(fresh_kernel, len(parts), first),
        out_shape=[
            shape,
            shape,
            jax.ShapeDtypeStruct((ranks, 2, page_rows, head_size), jnp.bfloat16),
        ],
        in_specs=[SCALARS] + [VECTORS] * (len(parts) + 2),
        out_specs=[VECTORS, VECTORS, ANY],
        scratch_shapes=[
            pltpu.VMEM((count, 2, page_rows, head_size), jnp.bfloat16),
            pltpu.SemaphoreType.DMA((count,)),
        ],
        compiler_params=PARAMS,
        cost_estimate=wait("fresh"),
        name="fresh_pages",
    )(numbers, *parts, cosine, sine)


def attend_kernel(terms, together, prefix, place, numbers, *refs):
    parts, (cosine, sine, keys_new, values_new) = refs[:terms], refs[terms : terms + 4]
    *pages, out, keys, values = refs[terms + 4 :]
    token_rows, head_size = keys_new.shape
    page_rows = pages[0].shape[2]
    group = out.shape[1] // head_size
    count = numbers[0, 0]
    scale = 1.0 / math.sqrt(head_size)

    def store(page, key, value):
        span = pl.ds(page * page_rows, page_rows)
        keys[span, :] = key
        values[span, :] = jnp.where(page < count, value, jnp.zeros_like(value))

    for page in range(prefix):
        owner = numbers[0, 1 + page]
        if len(pages) == 1:
            source = jnp.where(page < count, owner, 0)
            store(page, pages[0][source, 0], pages[0][source, 1])
        else:
            distance = place[0] ^ owner
            store(page, pages[0][0, 0], pages[0][0, 1])
            for index in range(2 * (len(pages) - 1)):
                source = (-1, index // 2) if index % 2 else (index // 2, 0)

                @pl.when(distance == index)
                def _(page=page, source=source):
                    taken = pages[source[0]]
                    store(page, taken[source[1], 0], taken[source[1], 1])

    keys[prefix * page_rows :, :] = keys_new[...]
    values[prefix * page_rows :, :] = values_new[...]
    total_rows = keys.shape[0]
    shape = (together * token_rows, total_rows)
    row = lax.broadcasted_iota(jnp.int32, shape, 0) % token_rows
    column = lax.broadcasted_iota(jnp.int32, shape, 1)
    new_column = column - prefix * page_rows
    allowed = (column < count * page_rows) | ((new_column >= 0) & (new_column <= row))
    for first in range(0, group, together):
        queries = []
        for member in range(first, first + together):
            lanes = pl.ds(member * head_size, head_size)
            total = sum(part[:token_rows, lanes].astype(jnp.float32) for part in parts)
            queries.append(turn(total, cosine[...], sine[...]).astype(jnp.bfloat16))
        queries = jnp.concatenate(queries, axis=0)
        scores = (
            lax.dot_general(
                queries, keys[...], (((1,), (1,)), ((), ())), preferred_element_type=jnp.float32
            )
            * scale
        )
        scores = jnp.where(allowed, scores, -1e30)
        largest = jnp.max(scores, axis=1, keepdims=True)
        weights = jnp.exp(scores - largest)
        totals = jnp.sum(weights, axis=1, keepdims=True)
        summed = jnp.dot(
            weights.astype(jnp.bfloat16), values[...], preferred_element_type=jnp.float32
        )
        result = (summed / totals).astype(out.dtype)
        for index in range(together):
            out[:, pl.ds((first + index) * head_size, head_size)] = result[
                index * token_rows : (index + 1) * token_rows
            ]


def attend(place, numbers, prefix, parts, cosine, sine, keys_new, values_new, pages):
    token_rows, head_size = cosine.shape
    group = parts[0].shape[1] // head_size
    total_rows = prefix * pages[0].shape[2] + token_rows
    together = group if total_rows <= 1024 else 1
    return pl.pallas_call(
        functools.partial(attend_kernel, len(parts), together, prefix),
        out_shape=jax.ShapeDtypeStruct((token_rows, group * head_size), jnp.bfloat16),
        in_specs=[SCALARS] * 2 + [VECTORS] * (len(parts) + 4 + len(pages)),
        out_specs=VECTORS,
        scratch_shapes=[pltpu.VMEM((total_rows, head_size), jnp.bfloat16)] * 2,
        compiler_params=PARAMS,
        cost_estimate=wait("attend"),
        name="attend",
    )(place, numbers, *parts, cosine, sine, keys_new, values_new, *pages)


def local(tokens, pool, pages_count, owners, slots, homes, home_slots, norm_attn, wqkv):
    ranks = lax.axis_size("dp")
    place = jnp.stack([lax.axis_index("dp"), lax.axis_index("tp")]).astype(jnp.int32)
    token_rows = tokens.shape[0]
    head_size = wqkv.shape[3]
    page_rows = pool.shape[2]
    prefix = owners.shape[1]
    new_pages = homes.shape[1]

    requests = [owners, slots, homes, home_slots]
    plan = column_plan if ranks == 8 else general_plan
    kv_parts, finish, table, copied, numbers = plan(
        tokens, norm_attn, wqkv, pages_count, requests, pool, place, ranks
    )
    positions = tie(pages_count[0], kv_parts[0]) * page_rows + jnp.arange(token_rows, dtype=jnp.int32)
    cosine, sine = rotary_tables(positions.astype(jnp.float32), head_size)
    keys_new, values_new, outgoing = fresh_pages(
        numbers, 1 + 2 * prefix, new_pages, kv_parts, cosine, sine, ranks, page_rows
    )
    incoming = lax.all_to_all(outgoing, "dp", split_axis=0, concat_axis=0, tiled=True)
    q_parts, pages = finish(keys_new)
    attended = attend(
        place, numbers, prefix, q_parts, cosine, sine, keys_new, values_new, pages
    )
    copied, attended = lax.optimization_barrier((copied, attended))
    pool_out = land_pages(table, incoming, copied)
    return (attended, pool_out)


def solution(mesh):
    in_specs = (
        P(("groups", "dp"), None),
        P(("groups", "dp"), None, None, "tp"),
        P(("groups", "dp")),
        P(("groups", "dp"), None),
        P(("groups", "dp"), None),
        P(("groups", "dp"), None),
        P(("groups", "dp"), None),
        P(),
        P("dp", "tp", None, None),
    )
    out_specs = (P(("groups", "dp"), "tp"), P(("groups", "dp"), None, None, "tp"))
    return jax.shard_map(local, mesh=mesh, in_specs=in_specs, out_specs=out_specs, check_vma=False)
```

```python
import functools
import math

import jax
import jax.numpy as jnp
from jax import lax
from jax.experimental import pallas as pl
from jax.experimental.pallas import tpu as pltpu
from jax.sharding import PartitionSpec as P

CFG = {'E': 'rec', 'P': [], 'Q': ['pick'], 'R': ['q'], 'G': ['pages'], 'X': ['fresh'], 'L': 0, 'W': 1, 'N': 0, 'V': 1, 'cost': {'prepare': 3, 'kv': 3, 'q': 0, 'fold': 0, 'pick': 10, 'fresh': 30, 'attend': 3, 'land': 3, 'relay': 10}}
ANY = pl.BlockSpec(memory_space=pl.ANY)
SCALARS = pl.BlockSpec(memory_space=pltpu.SMEM)
VECTORS = pl.BlockSpec(memory_space=pltpu.VMEM)
PARAMS = pltpu.CompilerParams(vmem_limit_bytes=32 * 1024 * 1024)


def wait(name):
    return pl.CostEstimate(flops=int(CFG['cost'].get(name, 0) * 1.15e9), bytes_accessed=0, transcendentals=0)


def tie(value, *others):
    return lax.optimization_barrier((value,) + others)[0]


def crossed(size, distance):
    return [(rank, rank ^ distance) for rank in range(size)]


def rotary_tables(positions, head_size):
    half_size = head_size // 2
    index_f = jnp.arange(half_size).astype(jnp.float32)
    inverse = jnp.exp(-(2.0 * index_f / head_size) * jnp.log(500000.0))
    angles = positions[:, None] * inverse[None, :]
    cosine, sine = jnp.cos(angles), jnp.sin(angles)
    return jnp.concatenate([cosine, cosine], axis=1), jnp.concatenate([-sine, sine], axis=1)


def turn(values, cosine, sine):
    return values * cosine + pltpu.roll(values, values.shape[-1] // 2, axis=1) * sine


def prepare_kernel(*refs):
    arguments, pieces, local_copies, semaphore = refs[:7], refs[7:12], refs[12:19], refs[19]
    copies = [
        pltpu.make_async_copy(here, there, semaphore.at[index])
        for index, (here, there) in enumerate(zip(arguments, local_copies))
    ]
    for copy in copies:
        copy.start()
    tokens, gain, pages_count, owners, slots, homes, home_slots = local_copies
    token_rows, width = tokens.shape
    rows = pieces[0].shape[1]
    member, core = lax.axis_index("dp") // 2, lax.axis_index("tp")
    for copy in copies:
        copy.wait()
    count = pages_count[0, 0]
    values = [count]
    values += [jnp.where(page < count, owners[0, page], -1) for page in range(owners.shape[1])]
    for ref in (slots, homes, home_slots):
        values += [ref[0, page] for page in range(ref.shape[1])]
    shape = (pieces[-1].shape[0] - token_rows, rows)
    column = lax.broadcasted_iota(jnp.int32, shape, 1)
    tail = jnp.zeros(shape, jnp.float32)
    for index, value in enumerate(values):
        tail = jnp.where(column == index, value.astype(jnp.float32), tail)
    wide = tokens[...].astype(jnp.float32)
    row_scale = lax.rsqrt(jnp.sum(wide * wide, axis=1, keepdims=True) / width + 1e-05)
    for index, piece in enumerate(pieces):
        target = member ^ max(index - 1, 0)
        half = 1 - core if index == 1 else core
        span = pl.ds(pl.multiple_of((2 * target + half) * rows, 128), rows)
        part = tokens[:, span].astype(jnp.float32) * row_scale * gain[:, span]
        piece[:token_rows] = part.astype(piece.dtype)
        piece[token_rows:] = tail.astype(piece.dtype)


def prepare(tokens, gain, pages_count, requests, rows):
    token_rows, width = tokens.shape
    arguments = [tokens, gain.reshape(1, width), pages_count.reshape(1, 1)] + requests
    return pl.pallas_call(
        prepare_kernel,
        out_shape=[jax.ShapeDtypeStruct((token_rows + 16, rows), jnp.bfloat16)] * 5,
        in_specs=[ANY] * 7,
        out_specs=[VECTORS] * 5,
        scratch_shapes=[pltpu.VMEM(value.shape, value.dtype) for value in arguments[:2]]
        + [pltpu.SMEM(value.shape, value.dtype) for value in arguments[2:]]
        + [pltpu.SemaphoreType.DMA((7,))],
        compiler_params=pltpu.CompilerParams(vmem_limit_bytes=60 * 1024 * 1024),
        cost_estimate=wait("prepare"),
        name="prepare",
    )(*arguments)


def side_by_side(*refs):
    return jnp.concatenate(
        [blocks[index] for blocks in refs for index in range(blocks.shape[0])], axis=1
    )


def product_kernel(place, *refs):
    weights = [ref for ref in refs[8:] if len(ref.shape) == 3]
    own, other = weights[: len(weights) // 2], weights[len(weights) // 2 :]
    kept, *leaving = refs[8 + len(weights) :]
    if len(leaving) == 4:
        table = leaving.pop()
        for index, ref in enumerate(refs[:4]):
            head = ref[kept.shape[0] : kept.shape[0] + 8, : table.shape[1]]
            table[index : index + 1] = head.astype(jnp.float32)[:1].astype(jnp.int32)
    rows = leaving[-1].shape[0] // (1 if len(leaving) == 3 else 2)
    direct = jnp.concatenate([ref[:rows] for ref in refs[:4]], axis=0)
    passed = jnp.concatenate([ref[:rows] for ref in refs[4:8]], axis=0)
    own_first = (place[0] % 2) == place[1]
    for_own = jnp.where(own_first, direct, passed)
    for_other = jnp.where(own_first, passed, direct)
    result = jnp.dot(
        for_own, side_by_side(*own), preferred_element_type=jnp.float32
    ) + jnp.dot(for_other, side_by_side(*other), preferred_element_type=jnp.float32)
    result = [result[index * rows : (index + 1) * rows] for index in range(4)]
    kept[:rows] = result[0]
    if len(leaving) == 3:
        for out, part in zip(leaving, result[1:]):
            out[...] = part.astype(out.dtype)
    else:
        kept[rows:] = result[2]
        leaving[0][:rows] = result[1].astype(leaving[0].dtype)
        leaving[0][rows:] = result[3].astype(leaving[0].dtype)


def products(place, direct, passed, own, other, paired):
    rows = direct[0].shape[0] - 16
    depth = 2 * own[0].shape[1]
    columns = sum(part.shape[0] * part.shape[2] for part in own)
    if paired:
        shapes = [((2 * rows, columns), jnp.float32), ((2 * rows, columns), jnp.bfloat16)]
    else:
        shapes = [((rows, columns), jnp.float32)] + [((rows, columns), jnp.bfloat16)] * 3
        shapes.append(((4, 128), jnp.int32))
    return pl.pallas_call(
        product_kernel,
        out_shape=[jax.ShapeDtypeStruct(shape, kind) for shape, kind in shapes],
        in_specs=[SCALARS] + [VECTORS] * (8 + 2 * len(own)),
        out_specs=[VECTORS] * len(shapes),
        compiler_params=PARAMS,
        cost_estimate=wait("q" if paired else "kv"),
        name="products",
    )(place, *direct, *passed, *own, *other)


def fold_kernel(kept, arrived, far):
    rows = far.shape[0]
    far[...] = (kept[rows:] + arrived[rows:].astype(jnp.float32)).astype(far.dtype)


def fold(kept, arrived):
    rows, columns = kept.shape[0] // 2, kept.shape[1]
    return pl.pallas_call(
        fold_kernel,
        out_shape=jax.ShapeDtypeStruct((rows, columns), jnp.bfloat16),
        in_specs=[VECTORS] * 2,
        out_specs=VECTORS,
        compiler_params=PARAMS,
        cost_estimate=wait("fold"),
        name="fold",
    )(kept, arrived)


def relay_kernel(*refs):
    for index, page in enumerate(refs[:4]):
        refs[4][index] = page[1]


def relay(pages):
    return pl.pallas_call(
        relay_kernel,
        out_shape=jax.ShapeDtypeStruct((4,) + pages[0].shape[1:], pages[0].dtype),
        in_specs=[VECTORS] * 4,
        out_specs=VECTORS,
        compiler_params=PARAMS,
        cost_estimate=wait("relay"),
        name="relay",
    )(*pages)


def near(values, ranks):
    return lax.ppermute(values, "dp", crossed(ranks, 1))


def along(values, ranks, step):
    return lax.ppermute(values, "dp", crossed(ranks, 2 * step))


def column_plan(tokens, gain, wqkv, pages_count, requests, pool, place, ranks):
    me = place[0]
    prefix = requests[0].shape[1]
    weight = wqkv[:, 0].transpose(1, 0, 2)
    own_direct, own_passed, *pieces = prepare(tokens, gain, pages_count, requests, wqkv.shape[0])
    if CFG["V"]:
        weight = tie(weight, pieces[0])
    *q_weight, kv_weight = [weight[first : first + 2] for first in range(0, weight.shape[0], 2)]
    kv_other, *q_other = [near(part, ranks) for part in [kv_weight] + q_weight]
    direct = [None] * 3
    for step in (2, 3, 1):
        direct[step - 1] = along(pieces[step - 1], ranks, step)
    if CFG["W"]:
        direct = tie(direct, kv_other)
    passed = [lax.ppermute(piece, "tp", crossed(2, 1)) for piece in direct]
    direct = [own_direct] + direct
    passed = [own_passed] + passed

    kv_own, *leaving, table = products(place, direct, passed, [kv_weight], [kv_other], False)
    kv_parts = [kv_own] + [along(part, ranks, step) for step, part in zip((1, 2, 3), leaving)]
    state = dict(kv=kv_own, kvp=kv_parts, kvd=kv_parts[1])
    get = lambda name: [state[k] for k in CFG[name]]

    def pick():
        t = [table, near(tie(table, *get("P")), ranks)]
        *picked, state["copied"] = pick_pages(place, t, pool, prefix)
        state["table"] = t
        state["pick"] = picked[0]
        state["pages"] = picked[:1] + [along(picked[step], ranks, step) for step in (1, 2, 3)]

    def q():
        w = tie(q_other, *get("Q"))
        state["q"], *leaving = products(place, direct, passed, q_weight, w, CFG["E"] == "rec")
        if CFG["E"] == "rec":
            state["qa"] = along(leaving[0], ranks, 1)
        else:
            state["qp"] = [state["q"]] + [along(p, ranks, i) for i, p in zip((1, 2, 3), leaving)]
            state["qa"] = state["qp"][1]

    if "pick" in CFG["Q"]:
        pick()
        q()
    else:
        q()
        pick()
    kv_parts = tie(kv_parts, *get("R"))

    def finish(fresh):
        state["fresh"] = fresh
        state["relay"] = tie(relay(state["pages"]), *get("X"))
        relayed = near(state["relay"], ranks)
        if CFG["E"] != "rec":
            return state["qp"], state["pages"] + [relayed], state["qa"]
        far = fold(state["q"], tie(state["qa"], *get("G")))
        state["far"] = far
        return [state["q"], state["qa"], along(far, ranks, 2)], state["pages"] + [relayed], far

    return kv_parts, finish, state["table"], state["copied"], table


def general_plan(tokens, gain, wqkv, pages_count, requests, pool, place, ranks):
    me = place[0]
    rows = wqkv.shape[0]
    members = ranks // 2
    token_rows = tokens.shape[0]
    blocks = wqkv.shape[2]
    prefix = requests[0].shape[1]
    weight = wqkv[:, 0].transpose(1, 0, 2)
    groups = [[2 * index + side for index in range(members)] for side in range(2)]
    wide = tokens.astype(jnp.float32)
    row_scale = lax.rsqrt(jnp.mean(wide * wide, axis=-1, keepdims=True) + 1e-05)
    normed = (wide * row_scale * gain).astype(jnp.bfloat16)
    chunks = normed.reshape(token_rows, members, 2 * rows).transpose(1, 0, 2)
    chunks = lax.all_to_all(
        chunks, "dp", split_axis=0, concat_axis=0, axis_index_groups=groups, tiled=True
    ).reshape(members * token_rows, 2 * rows)
    side = me % 2
    parts = jnp.dot(
        lax.dynamic_slice(chunks, (0, side * rows), (chunks.shape[0], rows)),
        side_by_side(weight),
        preferred_element_type=jnp.float32,
    ) + jnp.dot(
        lax.dynamic_slice(chunks, (0, (1 - side) * rows), (chunks.shape[0], rows)),
        side_by_side(near(weight, ranks)),
        preferred_element_type=jnp.float32,
    )
    parts = lax.all_to_all(
        parts.astype(jnp.bfloat16).reshape(members, token_rows, -1),
        "dp",
        split_axis=0,
        concat_axis=0,
        axis_index_groups=groups,
        tiled=True,
    )
    total = jnp.sum(parts.astype(jnp.float32), axis=0)
    q_columns = (blocks - 2) * wqkv.shape[3]
    listed = jnp.arange(prefix, dtype=jnp.int32) < pages_count[0]
    numbers = jnp.concatenate(
        [pages_count[:, None], jnp.where(listed, requests[0], -1)] + requests[1:], axis=1
    )
    table = [
        lax.all_to_all(
            jnp.broadcast_to(numbers, (ranks,) + numbers.shape[1:]),
            "dp",
            split_axis=0,
            concat_axis=0,
            tiled=True,
        )
    ]
    chosen, copied = pick_pages(place, table, pool, prefix)
    replies = lax.all_to_all(chosen, "dp", split_axis=0, concat_axis=0, tiled=True)

    def finish(fresh):
        return [total[:, :q_columns]], [replies], fresh

    return [total[:, q_columns:]], finish, table, copied, numbers


def each_row(tables, visit):
    base = 0
    for table in tables:
        rows = table.shape[0]
        if rows <= 8:
            for row in range(rows):
                visit(table, row, base + row)
        else:
            def step(row, carry, table=table, base=base):
                visit(table, row, base + row)
                return carry

            lax.fori_loop(0, rows, step, 0)
        base += rows


def slot_for(table, row, me, first, count):
    slot = jnp.int32(-1)
    for item in range(first, first + count):
        slot = jnp.where(table[row, item] == me, table[row, item + count], slot)
    return slot


def pick_kernel(count, prefix, place, *refs):
    tables, pool, copied, semaphore = refs[:count], refs[count], refs[-2], refs[-1]
    outs = refs[count + 1 : -2]
    whole = pltpu.make_async_copy(pool, copied, semaphore.at[semaphore.shape[0] - 1])
    whole.start()

    def visit(act, table, row, index):
        slot = slot_for(table, row, place[0], 1, prefix)

        @pl.when(slot >= 0)
        def _():
            target = outs[0].at[row] if count == 1 else outs[row].at[index // 4]
            act(pltpu.make_async_copy(pool.at[slot], target, semaphore.at[index]))

    each_row(tables, functools.partial(visit, lambda copy: copy.start()))
    each_row(tables, functools.partial(visit, lambda copy: copy.wait()))
    whole.wait()


def pick_pages(place, tables, pool, prefix):
    page = pool.shape[1:]
    rows = sum(table.shape[0] for table in tables)
    heights = [rows] if len(tables) == 1 else [len(tables)] * 4
    return pl.pallas_call(
        functools.partial(pick_kernel, len(tables), prefix),
        out_shape=[jax.ShapeDtypeStruct((height,) + page, pool.dtype) for height in heights]
        + [jax.ShapeDtypeStruct(pool.shape, pool.dtype)],
        in_specs=[SCALARS] * (1 + len(tables)) + [ANY],
        out_specs=[ANY] * (len(heights) + 1),
        scratch_shapes=[pltpu.SemaphoreType.DMA((rows + 1,))],
        compiler_params=PARAMS,
        cost_estimate=wait("pick"),
        name="pick_pages",
    )(place, *tables, pool)


def land_kernel(count, first, new_pages, place, *refs):
    tables, incoming, pool, semaphore = refs[:count], refs[count], refs[-2], refs[-1]

    def visit(act, table, row, index):
        slot = slot_for(table, row, place[0], first, new_pages)
        rank = row if count == 1 else place[0] ^ (2 * row + index // 4)

        @pl.when(slot >= 0)
        def _():
            act(pltpu.make_async_copy(incoming.at[rank], pool.at[slot], semaphore.at[index]))

    each_row(tables, functools.partial(visit, lambda copy: copy.start()))
    each_row(tables, functools.partial(visit, lambda copy: copy.wait()))


def land_pages(place, tables, incoming, pool, first, new_pages):
    ranks = incoming.shape[0]
    return pl.pallas_call(
        functools.partial(land_kernel, len(tables), first, new_pages),
        out_shape=jax.ShapeDtypeStruct(pool.shape, pool.dtype),
        in_specs=[SCALARS] * (1 + len(tables)) + [ANY, ANY],
        out_specs=ANY,
        scratch_shapes=[pltpu.SemaphoreType.DMA((ranks,))],
        input_output_aliases={2 + len(tables): 0},
        compiler_params=PARAMS,
        cost_estimate=wait("land"),
        name="land_pages",
    )(place, *tables, incoming, pool)


def fresh_kernel(pieces, first, numbers, *refs):
    parts = refs[:pieces]
    cosine, sine, keys, values, outgoing, pages, semaphore = refs[pieces:]
    token_rows, head_size = keys.shape
    total = sum(part[:token_rows].astype(jnp.float32) for part in parts)
    keys[...] = turn(total[:, :head_size], cosine[...], sine[...]).astype(keys.dtype)
    values[...] = total[:, head_size:].astype(values.dtype)
    count, _, page_rows, _ = pages.shape
    copies = []
    for page in range(count):
        span = pl.ds(page * page_rows, page_rows)
        pages[page, 0] = keys[span, :]
        pages[page, 1] = values[span, :]
        copies.append(
            pltpu.make_async_copy(
                pages.at[page], outgoing.at[numbers[0, first + page]], semaphore.at[page]
            )
        )
        copies[-1].start()
    for copy in copies:
        copy.wait()


def fresh_pages(numbers, first, count, parts, cosine, sine, ranks, page_rows):
    token_rows, head_size = cosine.shape
    shape = jax.ShapeDtypeStruct((token_rows, head_size), jnp.bfloat16)
    return pl.pallas_call(
        functools.partial(fresh_kernel, len(parts), first),
        out_shape=[
            shape,
            shape,
            jax.ShapeDtypeStruct((ranks, 2, page_rows, head_size), jnp.bfloat16),
        ],
        in_specs=[SCALARS] + [VECTORS] * (len(parts) + 2),
        out_specs=[VECTORS, VECTORS, ANY],
        scratch_shapes=[
            pltpu.VMEM((count, 2, page_rows, head_size), jnp.bfloat16),
            pltpu.SemaphoreType.DMA((count,)),
        ],
        compiler_params=PARAMS,
        cost_estimate=wait("fresh"),
        name="fresh_pages",
    )(numbers, *parts, cosine, sine)


def attend_kernel(terms, together, prefix, place, numbers, *refs):
    parts, (cosine, sine, keys_new, values_new) = refs[:terms], refs[terms : terms + 4]
    *pages, out, keys, values = refs[terms + 4 :]
    token_rows, head_size = keys_new.shape
    page_rows = pages[0].shape[2]
    group = out.shape[1] // head_size
    count = numbers[0, 0]
    scale = 1.0 / math.sqrt(head_size)

    def store(page, key, value):
        span = pl.ds(page * page_rows, page_rows)
        keys[span, :] = key
        values[span, :] = jnp.where(page < count, value, jnp.zeros_like(value))

    for page in range(prefix):
        owner = numbers[0, 1 + page]
        if len(pages) == 1:
            source = jnp.where(page < count, owner, 0)
            store(page, pages[0][source, 0], pages[0][source, 1])
        else:
            distance = place[0] ^ owner
            store(page, pages[0][0, 0], pages[0][0, 1])
            for index in range(2 * (len(pages) - 1)):
                source = (-1, index // 2) if index % 2 else (index // 2, 0)

                @pl.when(distance == index)
                def _(page=page, source=source):
                    taken = pages[source[0]]
                    store(page, taken[source[1], 0], taken[source[1], 1])

    keys[prefix * page_rows :, :] = keys_new[...]
    values[prefix * page_rows :, :] = values_new[...]
    total_rows = keys.shape[0]
    shape = (together * token_rows, total_rows)
    row = lax.broadcasted_iota(jnp.int32, shape, 0) % token_rows
    column = lax.broadcasted_iota(jnp.int32, shape, 1)
    new_column = column - prefix * page_rows
    allowed = (column < count * page_rows) | ((new_column >= 0) & (new_column <= row))
    for first in range(0, group, together):
        queries = []
        for member in range(first, first + together):
            lanes = pl.ds(member * head_size, head_size)
            total = sum(part[:token_rows, lanes].astype(jnp.float32) for part in parts)
            queries.append(turn(total, cosine[...], sine[...]).astype(jnp.bfloat16))
        queries = jnp.concatenate(queries, axis=0)
        scores = (
            lax.dot_general(
                queries, keys[...], (((1,), (1,)), ((), ())), preferred_element_type=jnp.float32
            )
            * scale
        )
        scores = jnp.where(allowed, scores, -1e30)
        largest = jnp.max(scores, axis=1, keepdims=True)
        weights = jnp.exp(scores - largest)
        totals = jnp.sum(weights, axis=1, keepdims=True)
        summed = jnp.dot(
            weights.astype(jnp.bfloat16), values[...], preferred_element_type=jnp.float32
        )
        result = (summed / totals).astype(out.dtype)
        for index in range(together):
            out[:, pl.ds((first + index) * head_size, head_size)] = result[
                index * token_rows : (index + 1) * token_rows
            ]


def attend(place, numbers, prefix, parts, cosine, sine, keys_new, values_new, pages):
    token_rows, head_size = cosine.shape
    group = parts[0].shape[1] // head_size
    total_rows = prefix * pages[0].shape[2] + token_rows
    together = group if total_rows <= 1024 else 1
    return pl.pallas_call(
        functools.partial(attend_kernel, len(parts), together, prefix),
        out_shape=jax.ShapeDtypeStruct((token_rows, group * head_size), jnp.bfloat16),
        in_specs=[SCALARS] * 2 + [VECTORS] * (len(parts) + 4 + len(pages)),
        out_specs=VECTORS,
        scratch_shapes=[pltpu.VMEM((total_rows, head_size), jnp.bfloat16)] * 2,
        compiler_params=PARAMS,
        cost_estimate=wait("attend"),
        name="attend",
    )(place, numbers, *parts, cosine, sine, keys_new, values_new, *pages)


def local(tokens, pool, pages_count, owners, slots, homes, home_slots, norm_attn, wqkv):
    ranks = lax.axis_size("dp")
    place = jnp.stack([lax.axis_index("dp"), lax.axis_index("tp")]).astype(jnp.int32)
    token_rows = tokens.shape[0]
    head_size = wqkv.shape[3]
    page_rows = pool.shape[2]
    prefix = owners.shape[1]
    new_pages = homes.shape[1]

    requests = [owners, slots, homes, home_slots]
    plan = column_plan if ranks == 8 else general_plan
    kv_parts, finish, table, copied, numbers = plan(
        tokens, norm_attn, wqkv, pages_count, requests, pool, place, ranks
    )
    positions = tie(pages_count[0], kv_parts[0]) * page_rows + jnp.arange(token_rows, dtype=jnp.int32)
    cosine, sine = rotary_tables(positions.astype(jnp.float32), head_size)
    keys_new, values_new, outgoing = fresh_pages(
        numbers, 1 + 2 * prefix, new_pages, kv_parts, cosine, sine, ranks, page_rows
    )
    q_parts, pages, far = finish(keys_new)
    if CFG["N"]:
        outgoing = tie(outgoing, far)
    incoming = lax.all_to_all(outgoing, "dp", split_axis=0, concat_axis=0, tiled=True)
    if CFG["L"] == 2:
        pool_out = land_pages(place, table, incoming, copied, 1 + 2 * prefix, new_pages)
        q_parts = tie(q_parts, pool_out)
    attended = attend(
        place, numbers, prefix, q_parts, cosine, sine, keys_new, values_new, pages
    )
    if CFG["L"] < 2:
        if CFG["L"]:
            copied, attended = lax.optimization_barrier((copied, attended))
        pool_out = land_pages(place, table, incoming, copied, 1 + 2 * prefix, new_pages)
    return (attended, pool_out)


def solution(mesh):
    in_specs = (
        P(("groups", "dp"), None),
        P(("groups", "dp"), None, None, "tp"),
        P(("groups", "dp")),
        P(("groups", "dp"), None),
        P(("groups", "dp"), None),
        P(("groups", "dp"), None),
        P(("groups", "dp"), None),
        P(),
        P("dp", "tp", None, None),
    )
    out_specs = (P(("groups", "dp"), "tp"), P(("groups", "dp"), None, None, "tp"))
    return jax.shard_map(local, mesh=mesh, in_specs=in_specs, out_specs=out_specs, check_vma=False)
```

```python
import functools
import math

import jax
import jax.numpy as jnp
from jax import lax
from jax.experimental import pallas as pl
from jax.experimental.pallas import tpu as pltpu
from jax.sharding import PartitionSpec as P

WAITS = {'prepare': 30, 'kv': 0, 'q': 1, 'settle': 10, 'relay': 0, 'pick': 10, 'fresh': 30, 'attend': 3, 'land': 0}
ANY = pl.BlockSpec(memory_space=pl.ANY)
SCALARS = pl.BlockSpec(memory_space=pltpu.SMEM)
VECTORS = pl.BlockSpec(memory_space=pltpu.VMEM)
PARAMS = pltpu.CompilerParams(vmem_limit_bytes=32 * 1024 * 1024)


def wait(name):
    return pl.CostEstimate(flops=int(WAITS[name] * 1.15e9), bytes_accessed=0, transcendentals=0)


def tie(value, *others):
    return lax.optimization_barrier((value,) + others)[0]


def crossed(size, distance):
    return [(rank, rank ^ distance) for rank in range(size)]


def rotary_tables(positions, head_size):
    half_size = head_size // 2
    index_f = jnp.arange(half_size).astype(jnp.float32)
    inverse = jnp.exp(-(2.0 * index_f / head_size) * jnp.log(500000.0))
    angles = positions[:, None] * inverse[None, :]
    cosine, sine = jnp.cos(angles), jnp.sin(angles)
    return jnp.concatenate([cosine, cosine], axis=1), jnp.concatenate([-sine, sine], axis=1)


def turn(values, cosine, sine):
    return values * cosine + pltpu.roll(values, values.shape[-1] // 2, axis=1) * sine


def prepare_kernel(*refs):
    arguments, pieces, local_copies, semaphore = refs[:7], refs[7:12], refs[12:19], refs[19]
    copies = [
        pltpu.make_async_copy(here, there, semaphore.at[index])
        for index, (here, there) in enumerate(zip(arguments, local_copies))
    ]
    for copy in copies:
        copy.start()
    tokens, gain, pages_count, owners, slots, homes, home_slots = local_copies
    token_rows, width = tokens.shape
    rows = pieces[0].shape[1]
    member, core = lax.axis_index("dp") // 2, lax.axis_index("tp")
    for copy in copies:
        copy.wait()
    count = pages_count[0, 0]
    values = [count]
    values += [jnp.where(page < count, owners[0, page], -1) for page in range(owners.shape[1])]
    for ref in (slots, homes, home_slots):
        values += [ref[0, page] for page in range(ref.shape[1])]
    shape = (pieces[-1].shape[0] - token_rows, rows)
    column = lax.broadcasted_iota(jnp.int32, shape, 1)
    tail = jnp.zeros(shape, jnp.float32)
    for index, value in enumerate(values):
        tail = jnp.where(column == index, value.astype(jnp.float32), tail)
    wide = tokens[...].astype(jnp.float32)
    row_scale = lax.rsqrt(jnp.sum(wide * wide, axis=1, keepdims=True) / width + 1e-05)
    for index, piece in enumerate(pieces):
        target = member ^ max(index - 1, 0)
        half = 1 - core if index == 1 else core
        span = pl.ds(pl.multiple_of((2 * target + half) * rows, 128), rows)
        part = tokens[:, span].astype(jnp.float32) * row_scale * gain[:, span]
        piece[:token_rows] = part.astype(piece.dtype)
        piece[token_rows:] = tail.astype(piece.dtype)


def prepare(tokens, gain, pages_count, requests, rows):
    token_rows, width = tokens.shape
    arguments = [tokens, gain.reshape(1, width), pages_count.reshape(1, 1)] + requests
    return pl.pallas_call(
        prepare_kernel,
        out_shape=[jax.ShapeDtypeStruct((token_rows + 16, rows), jnp.bfloat16)] * 5,
        in_specs=[ANY] * 7,
        out_specs=[VECTORS] * 5,
        scratch_shapes=[pltpu.VMEM(value.shape, value.dtype) for value in arguments[:2]]
        + [pltpu.SMEM(value.shape, value.dtype) for value in arguments[2:]]
        + [pltpu.SemaphoreType.DMA((7,))],
        compiler_params=pltpu.CompilerParams(vmem_limit_bytes=60 * 1024 * 1024),
        cost_estimate=wait("prepare"),
        name="prepare",
    )(*arguments)


def side_by_side(*refs):
    return jnp.concatenate(
        [blocks[index] for blocks in refs for index in range(blocks.shape[0])], axis=1
    )


def multiply(place, tokens, weights, rows):
    direct = jnp.concatenate([ref[:rows] for ref in tokens[:4]], axis=0)
    passed = jnp.concatenate([ref[:rows] for ref in tokens[4:]], axis=0)
    own, other = weights[: len(weights) // 2], weights[len(weights) // 2 :]
    own_first = (place[0] % 2) == place[1]
    for_own = jnp.where(own_first, direct, passed)
    for_other = jnp.where(own_first, passed, direct)
    result = jnp.dot(
        for_own, side_by_side(*own), preferred_element_type=jnp.float32
    ) + jnp.dot(for_other, side_by_side(*other), preferred_element_type=jnp.float32)
    return [result[index * rows : (index + 1) * rows] for index in range(4)]


def kv_kernel(place, *refs):
    tokens, weights, (kept, *leaving), table = refs[:8], refs[8:10], refs[10:14], refs[14]
    for index, ref in enumerate(tokens[:4]):
        head = ref[kept.shape[0] : kept.shape[0] + 8, : table.shape[1]]
        table[index : index + 1] = head.astype(jnp.float32)[:1].astype(jnp.int32)
    parts = multiply(place, tokens, weights, kept.shape[0])
    for out, part in zip((kept, *leaving), parts):
        out[...] = part.astype(out.dtype)


def kv_products(place, tokens, own, other):
    rows = tokens[0].shape[0] - 16
    columns = own.shape[0] * own.shape[2]
    return pl.pallas_call(
        kv_kernel,
        out_shape=[jax.ShapeDtypeStruct((rows, columns), jnp.float32)]
        + [jax.ShapeDtypeStruct((rows, columns), jnp.bfloat16)] * 3
        + [jax.ShapeDtypeStruct((4, 128), jnp.int32)],
        in_specs=[SCALARS] + [VECTORS] * 10,
        out_specs=[VECTORS] * 5,
        compiler_params=PARAMS,
        cost_estimate=wait("kv"),
        name="kv_products",
    )(place, *tokens, own, other)


def q_kernel(place, *refs):
    tokens, weights, kept, leaving = refs[:8], refs[8:-2], refs[-2], refs[-1]
    rows = kept.shape[0] // 2
    parts = multiply(place, tokens, weights, rows)
    kept[:rows], kept[rows:] = parts[0], parts[2]
    leaving[:rows] = parts[1].astype(leaving.dtype)
    leaving[rows:] = parts[3].astype(leaving.dtype)


def q_products(place, tokens, own, other):
    rows = tokens[0].shape[0] - 16
    columns = sum(part.shape[0] * part.shape[2] for part in own)
    return pl.pallas_call(
        q_kernel,
        out_shape=[
            jax.ShapeDtypeStruct((2 * rows, columns), kind) for kind in (jnp.float32, jnp.bfloat16)
        ],
        in_specs=[SCALARS] + [VECTORS] * (8 + 2 * len(own)),
        out_specs=[VECTORS] * 2,
        compiler_params=PARAMS,
        cost_estimate=wait("q"),
        name="q_products",
    )(place, *tokens, *own, *other)


def choose_kernel(prefix, place, *refs):
    tables, pool, outs, copied, semaphore = refs[:2], refs[2], refs[3:7], refs[7], refs[8]
    page_rows = pool.shape[2]
    whole = pltpu.make_async_copy(pool, copied, semaphore.at[16])
    whole.start()

    def visit(act, table, row, index):
        slot = slot_for(table, row, place[0], 1, prefix)

        @pl.when(slot >= 0)
        def _():
            for half in range(2):
                target = outs[row].at[pl.ds((2 * (index // 4) + half) * page_rows, page_rows)]
                act(
                    pltpu.make_async_copy(
                        pool.at[slot, half], target, semaphore.at[2 * index + half]
                    )
                )

    each_row(tables, functools.partial(visit, lambda copy: copy.start()))
    each_row(tables, functools.partial(visit, lambda copy: copy.wait()))
    whole.wait()


def choose_pages(place, tables, pool, prefix):
    pages = jax.ShapeDtypeStruct((4 * pool.shape[2], pool.shape[3]), pool.dtype)
    return pl.pallas_call(
        functools.partial(choose_kernel, prefix),
        out_shape=[pages] * 4 + [jax.ShapeDtypeStruct(pool.shape, pool.dtype)],
        in_specs=[SCALARS] * 3 + [ANY],
        out_specs=[VECTORS] * 4 + [ANY],
        scratch_shapes=[pltpu.SemaphoreType.DMA((17,))],
        compiler_params=PARAMS,
        cost_estimate=wait("pick"),
        name="choose_pages",
    )(place, *tables, pool)


def fold_kernel(kept, arrived, far):
    rows = far.shape[0]
    far[...] = (kept[rows:] + arrived[rows:].astype(jnp.float32)).astype(far.dtype)


def fold(kept, arrived):
    rows, columns = kept.shape[0] // 2, kept.shape[1]
    return pl.pallas_call(
        fold_kernel,
        out_shape=jax.ShapeDtypeStruct((rows, columns), jnp.bfloat16),
        in_specs=[VECTORS] * 2,
        out_specs=VECTORS,
        compiler_params=PARAMS,
        cost_estimate=wait("settle"),
        name="fold",
    )(kept, arrived)


def relay_kernel(*refs):
    rows = refs[4].shape[0] // 4
    for index, page in enumerate(refs[:4]):
        refs[4][index * rows : (index + 1) * rows] = page[rows:]


def relay(pages):
    return pl.pallas_call(
        relay_kernel,
        out_shape=jax.ShapeDtypeStruct((2 * pages[0].shape[0], pages[0].shape[1]), pages[0].dtype),
        in_specs=[VECTORS] * 4,
        out_specs=VECTORS,
        compiler_params=PARAMS,
        cost_estimate=wait("relay"),
        name="relay",
    )(*pages)


def near(values, ranks):
    return lax.ppermute(values, "dp", crossed(ranks, 1))


def along(values, ranks, step):
    return lax.ppermute(values, "dp", crossed(ranks, 2 * step))


def column_plan(tokens, gain, wqkv, pages_count, requests, pool, place, ranks):
    prefix = requests[0].shape[1]
    own_direct, own_passed, *pieces = prepare(tokens, gain, pages_count, requests, wqkv.shape[0])
    weight = tie(wqkv[:, 0].transpose(1, 0, 2), pieces[0])
    *q_weight, kv_weight = [weight[first : first + 2] for first in range(0, weight.shape[0], 2)]
    kv_other, *q_other = [near(part, ranks) for part in [kv_weight] + q_weight]
    direct = [None] * 3
    for step in (2, 3, 1):
        direct[step - 1] = along(pieces[step - 1], ranks, step)
    passed = [lax.ppermute(piece, "tp", crossed(2, 1)) for piece in direct]
    sources = [own_direct, *direct, own_passed, *passed]

    kv_own, *leaving, table = kv_products(place, sources, kv_weight, kv_other)
    kv_parts = [kv_own] + [along(part, ranks, step) for step, part in zip((1, 2, 3), leaving)]
    tables = [table, near(table, ranks)]
    q_kept, leaving = q_products(place, sources, q_weight, tie(q_other, kv_own))
    arrived = along(leaving, ranks, 1)
    *chosen, copied = choose_pages(place, tie(tables, q_kept), pool, prefix)
    pages = chosen[:1] + [along(chosen[step], ranks, step) for step in (1, 2, 3)]
    kv_parts = tie(kv_parts, q_kept)

    def finish(fresh):
        far = fold(q_kept, tie(arrived, fresh))
        passed_on = relay(pages)
        terms = [q_kept, arrived, along(far, ranks, 2)]
        return terms, pages + [near(passed_on, ranks)], copied

    return kv_parts, finish, tables, table


def general_plan(tokens, gain, wqkv, pages_count, requests, pool, place, ranks):
    me = place[0]
    rows = wqkv.shape[0]
    members = ranks // 2
    token_rows = tokens.shape[0]
    blocks = wqkv.shape[2]
    prefix = requests[0].shape[1]
    weight = wqkv[:, 0].transpose(1, 0, 2)
    groups = [[2 * index + side for index in range(members)] for side in range(2)]
    wide = tokens.astype(jnp.float32)
    row_scale = lax.rsqrt(jnp.mean(wide * wide, axis=-1, keepdims=True) + 1e-05)
    normed = (wide * row_scale * gain).astype(jnp.bfloat16)
    chunks = normed.reshape(token_rows, members, 2 * rows).transpose(1, 0, 2)
    chunks = lax.all_to_all(
        chunks, "dp", split_axis=0, concat_axis=0, axis_index_groups=groups, tiled=True
    ).reshape(members * token_rows, 2 * rows)
    side = me % 2
    parts = jnp.dot(
        lax.dynamic_slice(chunks, (0, side * rows), (chunks.shape[0], rows)),
        side_by_side(weight),
        preferred_element_type=jnp.float32,
    ) + jnp.dot(
        lax.dynamic_slice(chunks, (0, (1 - side) * rows), (chunks.shape[0], rows)),
        side_by_side(near(weight, ranks)),
        preferred_element_type=jnp.float32,
    )
    parts = lax.all_to_all(
        parts.astype(jnp.bfloat16).reshape(members, token_rows, -1),
        "dp",
        split_axis=0,
        concat_axis=0,
        axis_index_groups=groups,
        tiled=True,
    )
    total = jnp.sum(parts.astype(jnp.float32), axis=0)
    q_columns = (blocks - 2) * wqkv.shape[3]
    listed = jnp.arange(prefix, dtype=jnp.int32) < pages_count[0]
    numbers = jnp.concatenate(
        [pages_count[:, None], jnp.where(listed, requests[0], -1)] + requests[1:], axis=1
    )
    table = [
        lax.all_to_all(
            jnp.broadcast_to(numbers, (ranks,) + numbers.shape[1:]),
            "dp",
            split_axis=0,
            concat_axis=0,
            tiled=True,
        )
    ]
    chosen, copied = pick_pages(place, table[0], pool, prefix)
    replies = lax.all_to_all(chosen, "dp", split_axis=0, concat_axis=0, tiled=True)

    def finish(fresh):
        return [total[:, :q_columns]], [replies], copied

    return [total[:, q_columns:]], finish, table, numbers


def each_row(tables, visit):
    base = 0
    for table in tables:
        rows = table.shape[0]
        if rows <= 8:
            for row in range(rows):
                visit(table, row, base + row)
        else:
            def step(row, carry, table=table, base=base):
                visit(table, row, base + row)
                return carry

            lax.fori_loop(0, rows, step, 0)
        base += rows


def slot_for(table, row, me, first, count):
    slot = jnp.int32(-1)
    for item in range(first, first + count):
        slot = jnp.where(table[row, item] == me, table[row, item + count], slot)
    return slot


def pick_kernel(prefix, place, table, pool, chosen, copied, semaphore):
    whole = pltpu.make_async_copy(pool, copied, semaphore.at[table.shape[0]])
    whole.start()

    def visit(act, table, row, index):
        slot = slot_for(table, row, place[0], 1, prefix)

        @pl.when(slot >= 0)
        def _():
            act(pltpu.make_async_copy(pool.at[slot], chosen.at[row], semaphore.at[index]))

    each_row([table], functools.partial(visit, lambda copy: copy.start()))
    each_row([table], functools.partial(visit, lambda copy: copy.wait()))
    whole.wait()


def pick_pages(place, table, pool, prefix):
    rows = table.shape[0]
    return pl.pallas_call(
        functools.partial(pick_kernel, prefix),
        out_shape=[
            jax.ShapeDtypeStruct((rows,) + pool.shape[1:], pool.dtype),
            jax.ShapeDtypeStruct(pool.shape, pool.dtype),
        ],
        in_specs=[SCALARS] * 2 + [ANY],
        out_specs=[ANY] * 2,
        scratch_shapes=[pltpu.SemaphoreType.DMA((rows + 1,))],
        compiler_params=PARAMS,
        cost_estimate=wait("pick"),
        name="pick_pages",
    )(place, table, pool)


def land_kernel(count, first, new_pages, place, *refs):
    tables, incoming, pool, semaphore = refs[:count], refs[count], refs[-2], refs[-1]

    def visit(act, table, row, index):
        slot = slot_for(table, row, place[0], first, new_pages)
        rank = row if count == 1 else place[0] ^ (2 * row + index // 4)

        @pl.when(slot >= 0)
        def _():
            act(pltpu.make_async_copy(incoming.at[rank], pool.at[slot], semaphore.at[index]))

    each_row(tables, functools.partial(visit, lambda copy: copy.start()))
    each_row(tables, functools.partial(visit, lambda copy: copy.wait()))


def land_pages(place, tables, incoming, pool, first, new_pages):
    ranks = incoming.shape[0]
    return pl.pallas_call(
        functools.partial(land_kernel, len(tables), first, new_pages),
        out_shape=jax.ShapeDtypeStruct(pool.shape, pool.dtype),
        in_specs=[SCALARS] * (1 + len(tables)) + [ANY, ANY],
        out_specs=ANY,
        scratch_shapes=[pltpu.SemaphoreType.DMA((ranks,))],
        input_output_aliases={2 + len(tables): 0},
        compiler_params=PARAMS,
        cost_estimate=wait("land"),
        name="land_pages",
    )(place, *tables, incoming, pool)


def fresh_kernel(pieces, first, numbers, *refs):
    parts = refs[:pieces]
    cosine, sine, keys, values, outgoing = refs[pieces:]
    token_rows, head_size = keys.shape
    total = sum(part[:token_rows].astype(jnp.float32) for part in parts)
    keys[...] = turn(total[:, :head_size], cosine[...], sine[...]).astype(keys.dtype)
    values[...] = total[:, head_size:].astype(values.dtype)
    page_rows = outgoing.shape[2]
    for page in range(keys.shape[0] // page_rows):
        span = pl.ds(page * page_rows, page_rows)
        home = numbers[0, first + page]
        outgoing[home, 0] = keys[span, :]
        outgoing[home, 1] = values[span, :]


def fresh_pages(numbers, first, parts, cosine, sine, ranks, page_rows):
    token_rows, head_size = cosine.shape
    shape = jax.ShapeDtypeStruct((token_rows, head_size), jnp.bfloat16)
    return pl.pallas_call(
        functools.partial(fresh_kernel, len(parts), first),
        out_shape=[
            shape,
            shape,
            jax.ShapeDtypeStruct((ranks, 2, page_rows, head_size), jnp.bfloat16),
        ],
        in_specs=[SCALARS] + [VECTORS] * (len(parts) + 2),
        out_specs=[VECTORS] * 3,
        compiler_params=PARAMS,
        cost_estimate=wait("fresh"),
        name="fresh_pages",
    )(numbers, *parts, cosine, sine)


def attend_kernel(terms, together, prefix, place, numbers, *refs):
    parts, (cosine, sine, keys_new, values_new) = refs[:terms], refs[terms : terms + 4]
    *pages, out, keys, values = refs[terms + 4 :]
    token_rows, head_size = keys_new.shape
    page_rows = (keys.shape[0] - token_rows) // prefix
    group = out.shape[1] // head_size
    count = numbers[0, 0]
    scale = 1.0 / math.sqrt(head_size)

    def store(page, key, value):
        span = pl.ds(page * page_rows, page_rows)
        keys[span, :] = key
        values[span, :] = jnp.where(page < count, value, jnp.zeros_like(value))

    def take(page, source, first):
        columns = slice(source.shape[1] - head_size, source.shape[1])
        middle = first + page_rows
        store(page, source[first:middle, columns], source[middle : middle + page_rows, columns])

    for page in range(prefix):
        owner = numbers[0, 1 + page]
        if len(pages) == 1:
            source = jnp.where(page < count, owner, 0)
            store(page, pages[0][source, 0], pages[0][source, 1])
        else:
            distance = place[0] ^ owner
            take(page, pages[0], 0)
            for index in range(1, 2 * (len(pages) - 1)):
                source = (-1, index // 2) if index % 2 else (index // 2, 0)

                @pl.when(distance == index)
                def _(page=page, source=source):
                    take(page, pages[source[0]], 2 * page_rows * source[1])

    keys[prefix * page_rows :, :] = keys_new[...]
    values[prefix * page_rows :, :] = values_new[...]
    total_rows = keys.shape[0]
    shape = (together * token_rows, total_rows)
    row = lax.broadcasted_iota(jnp.int32, shape, 0) % token_rows
    column = lax.broadcasted_iota(jnp.int32, shape, 1)
    new_column = column - prefix * page_rows
    allowed = (column < count * page_rows) | ((new_column >= 0) & (new_column <= row))
    for first in range(0, group, together):
        queries = []
        for member in range(first, first + together):
            lanes = pl.ds(member * head_size, head_size)
            total = sum(part[:token_rows, lanes].astype(jnp.float32) for part in parts)
            queries.append(turn(total, cosine[...], sine[...]).astype(jnp.bfloat16))
        queries = jnp.concatenate(queries, axis=0)
        scores = (
            lax.dot_general(
                queries, keys[...], (((1,), (1,)), ((), ())), preferred_element_type=jnp.float32
            )
            * scale
        )
        scores = jnp.where(allowed, scores, -1e30)
        largest = jnp.max(scores, axis=1, keepdims=True)
        weights = jnp.exp(scores - largest)
        totals = jnp.sum(weights, axis=1, keepdims=True)
        summed = jnp.dot(
            weights.astype(jnp.bfloat16), values[...], preferred_element_type=jnp.float32
        )
        result = (summed / totals).astype(out.dtype)
        for index in range(together):
            out[:, pl.ds((first + index) * head_size, head_size)] = result[
                index * token_rows : (index + 1) * token_rows
            ]


def attend(place, numbers, prefix, page_rows, parts, cosine, sine, keys_new, values_new, pages):
    token_rows, head_size = cosine.shape
    group = parts[0].shape[1] // head_size
    total_rows = prefix * page_rows + token_rows
    together = group if total_rows <= 1024 else 1
    return pl.pallas_call(
        functools.partial(attend_kernel, len(parts), together, prefix),
        out_shape=jax.ShapeDtypeStruct((token_rows, group * head_size), jnp.bfloat16),
        in_specs=[SCALARS] * 2 + [VECTORS] * (len(parts) + 4 + len(pages)),
        out_specs=VECTORS,
        scratch_shapes=[pltpu.VMEM((total_rows, head_size), jnp.bfloat16)] * 2,
        compiler_params=PARAMS,
        cost_estimate=wait("attend"),
        name="attend",
    )(place, numbers, *parts, cosine, sine, keys_new, values_new, *pages)


def local(tokens, pool, pages_count, owners, slots, homes, home_slots, norm_attn, wqkv):
    ranks = lax.axis_size("dp")
    place = jnp.stack([lax.axis_index("dp"), lax.axis_index("tp")]).astype(jnp.int32)
    token_rows = tokens.shape[0]
    head_size = wqkv.shape[3]
    page_rows = pool.shape[2]
    prefix = owners.shape[1]
    new_pages = homes.shape[1]

    requests = [owners, slots, homes, home_slots]
    plan = column_plan if ranks == 8 else general_plan
    kv_parts, finish, tables, numbers = plan(
        tokens, norm_attn, wqkv, pages_count, requests, pool, place, ranks
    )
    positions = tie(pages_count[0], kv_parts[0]) * page_rows + jnp.arange(token_rows, dtype=jnp.int32)
    cosine, sine = rotary_tables(positions.astype(jnp.float32), head_size)
    keys_new, values_new, outgoing = fresh_pages(
        numbers, 1 + 2 * prefix, kv_parts, cosine, sine, ranks, page_rows
    )
    incoming = lax.all_to_all(outgoing, "dp", split_axis=0, concat_axis=0, tiled=True)
    q_parts, pages, copied = finish(keys_new)
    pool_out = land_pages(place, tables, incoming, copied, 1 + 2 * prefix, new_pages)
    q_parts = tie(q_parts, pool_out)
    attended = attend(
        place, numbers, prefix, page_rows, q_parts, cosine, sine, keys_new, values_new, pages
    )
    return (attended, pool_out)


def solution(mesh):
    in_specs = (
        P(("groups", "dp"), None),
        P(("groups", "dp"), None, None, "tp"),
        P(("groups", "dp")),
        P(("groups", "dp"), None),
        P(("groups", "dp"), None),
        P(("groups", "dp"), None),
        P(("groups", "dp"), None),
        P(),
        P("dp", "tp", None, None),
    )
    out_specs = (P(("groups", "dp"), "tp"), P(("groups", "dp"), None, None, "tp"))
    return jax.shard_map(local, mesh=mesh, in_specs=in_specs, out_specs=out_specs, check_vma=False)
```
